256 devices in a mesh: seq: 32 (over x, z), head: 8 (over y, core).
Axes of the slice: x: 4, y: 4, z: 8, core: 2. Of those that a mesh axis runs over, the one named last changes fastest.
Arguments:
- tokens: bfloat16 [8192, 2048], P(('seq', 'head')), may hold values from -6 to 6
- w_query: bfloat16 [2048, 2048], P(None, 'head'), may hold values from -0.125 to 0.125
- w_key: bfloat16 [2048, 2048], P(None, 'head'), may hold values from -1 to 1
- w_value: bfloat16 [2048, 4096], P(None, 'head'), may hold values from -0.125 to 0.125
- w_beta: bfloat16 [2048, 32], P(None, 'head'), may hold values from -0.1875 to 0.1875
- w_out: bfloat16 [4096, 2048], P('head'), may hold values from -0.09375 to 0.09375
- mask_query: int32 [32, 32], P(None, 'head'), may hold values 0 or 1
- mask_key: int32 [32, 32], P(None, 'head'), may hold values 0 or 1
- mask_value: int32 [32, 64], P(None, 'head'), may hold values 0 or 1
- mask_out: int32 [64, 32], P('head'), may hold values 0 or 1
- decay_rate: float32 [8192, 32], P('seq', 'head'), may hold values from 0.9 to 0.999999
- norm_gain: float32 [128], replicated, may hold values from 0.1 to 1.9
Outputs:
- mixed_out: bfloat16 [8192, 2048], P(('seq', 'head'))
The draws below stay inside these ranges and needn't reach their ends.
Inputs may be any that keep to these rules, and one draw needn't show every extreme that they name: `mask_query`: 1 keeps a 64 x 64 weight block, 0 prunes it. `mask_key`: 1 keeps a 64 x 64 weight block, 0 prunes it. `mask_value`: 1 keeps a 64 x 64 weight block, 0 prunes it. `mask_out`: 1 keeps a 64 x 64 weight block, 0 prunes it.
All inputs are finite; a program needn't handle non-finite values.
Results may differ from the reference program's by a relative error of at most 0.029.
Values may be sent and summed in bfloat16 or wider, within the bound.
A program may use at most 128 MiB of HBM per device.

```python
import math
import jax
import jax.numpy as jnp
from jax import lax

D = 2048
KH = 16
VH = 32
HD = 128
TOK_DEV = 256
BLOCK_LEN = 64
TILE = 64
TOKENS = 8192


def draw_decay_rate(key, part):
    key = jax.random.fold_in(key, 7)
    pick_key, level_key, shard_key, jitter_key, spot_key, fast_key = jax.random.split(key, 6)
    fast_share = 0.5
    slow_low = 0.2
    slow_high = 1.0
    slow_rate = jnp.exp(jax.random.uniform(level_key, (1, VH), jnp.float32, math.log(slow_low), math.log(slow_high))) * (1.0 / TOKENS)
    fast_rate = jnp.exp(jax.random.uniform(fast_key, (1, VH), jnp.float32, math.log(1.0 / 50.0), math.log(1.0 / 30.0)))
    is_fast = jax.random.uniform(pick_key, (1, VH), jnp.float32) < fast_share
    base_rate = jnp.where(is_fast, fast_rate, slow_rate)
    shard_factor = jnp.exp(jax.random.uniform(shard_key, (TOKENS // TOK_DEV, 1, VH), jnp.float32, -0.69, 0.69))
    shard_factor = jnp.broadcast_to(shard_factor, (TOKENS // TOK_DEV, TOK_DEV, VH)).reshape(TOKENS, VH)
    jitter = jnp.exp(jax.random.uniform(jitter_key, (TOKENS, VH), jnp.float32, -0.69, 0.69))
    starts = jax.random.randint(spot_key, (2, 1, VH), 0, TOKENS - 2)
    places = jnp.arange(TOKENS, dtype=jnp.int32)[None, :, None]
    inside = jnp.any((places >= starts) & (places < starts + 3), axis=0)
    loss_rates = jnp.where(inside, 0.1, base_rate * shard_factor * jitter)
    return jnp.clip(1.0 - loss_rates, 0.9, 0.999999).astype(jnp.float32)


def draw_w_key(key, part):
    key = jax.random.fold_in(key, 11)
    entry_key, scale_key, turn_key = jax.random.split(key, 3)
    entries = jnp.clip(jax.random.normal(entry_key, (D, KH, HD), jnp.float32), -4.0, 4.0)
    lowest = 0.5 * math.log(HD / (8.0 * TOKENS))
    column_scale = jnp.exp(jax.random.uniform(scale_key, (1, KH, HD), jnp.float32, lowest, 0.0))
    rotated = entries * column_scale * (1.0 / math.sqrt(D))
    half_width = 1
    section_index = 0
    while 2 * half_width <= TILE and TILE % (2 * half_width) == 0 and (HD % (2 * half_width) == 0):
        groups = HD // (2 * half_width)
        turn_angle = jax.random.uniform(jax.random.fold_in(turn_key, section_index), (1, KH, groups, 1, half_width), jnp.float32, -math.pi, math.pi)
        grouped = rotated.reshape(D, KH, groups, 2, half_width)
        upper_part = grouped[:, :, :, 0:1, :]
        lower_part = grouped[:, :, :, 1:2, :]
        cosine = jnp.cos(turn_angle)
        sine_part = jnp.sin(turn_angle)
        rotated = jnp.concatenate([cosine * upper_part - sine_part * lower_part, sine_part * upper_part + cosine * lower_part], 3).reshape(D, KH, HD)
        half_width = half_width * 2
        section_index = section_index + 1
    return jnp.clip(rotated, -1.0, 1.0).reshape(D, KH * HD).astype(jnp.bfloat16)


def with_ends(values, key, least, top_value):
    longest = values.shape.index(max(values.shape))
    spots = []
    for shift in (0, 1):
        where = [jax.random.randint(jax.random.fold_in(key, axis), (), 0, length) for axis, length in enumerate(values.shape)]
        where[longest] = (where[longest] + shift) % values.shape[longest]
        spots.append(tuple(where))
    return values.at[spots[0]].set(least).at[spots[1]].set(top_value)


def block_scale(own_key, dims, shards, least, high):
    gain = 1.0
    for axis_at, blocks in shards:
        heights = jax.random.uniform(jax.random.fold_in(jax.random.fold_in(own_key, 6), axis_at), (blocks,), jnp.float32, least / len(shards), high / len(shards))
        gain = gain * jnp.repeat(jnp.exp(heights), dims[axis_at] // blocks).reshape((-1,) + (1,) * (len(dims) - 1 - axis_at))
    return gain


def noise(stream_key, dims, scale, bound, pieces=(), held_as=jnp.bfloat16):
    level = block_scale(stream_key, dims, pieces, -0.22, 0.18) if pieces else 1.0
    values = jax.random.normal(stream_key, dims, jnp.float32) * scale * level
    return jnp.minimum(jnp.maximum(values, -bound), bound).astype(held_as)


def setup_inputs(seed: int = 0) -> dict:
    splits = jax.random.split(jax.random.key(seed), 13)
    tokens = noise(splits[0], (TOKENS, D), 1.0, 6.0, ((0, 256),))
    w_query = noise(splits[1], (D, KH * HD), D ** -0.5, 0.125, ((1, 8),))
    w_key = draw_w_key(jax.random.fold_in(splits[12], 71), 0)
    w_value = noise(splits[3], (D, VH * HD), D ** -0.5, 0.125, ((1, 8),))
    w_beta = noise(splits[4], (D, VH), (D // 2) ** -0.5, 0.1875, ((1, 8),))
    w_out = noise(splits[5], (VH * HD, D), (VH * HD) ** -0.5, 0.09375, ((0, 8),))
    mask_query = with_ends((jax.random.randint(splits[6], (D // TILE, KH * HD // TILE), 0, 4) < 3).astype(jnp.int32), jax.random.fold_in(splits[6], 1), 0, 1)
    mask_key = with_ends((jax.random.randint(splits[7], (D // TILE, KH * HD // TILE), 0, 4) < 3).astype(jnp.int32), jax.random.fold_in(splits[7], 1), 0, 1)
    mask_value = with_ends((jax.random.randint(splits[8], (D // TILE, VH * HD // TILE), 0, 4) < 3).astype(jnp.int32), jax.random.fold_in(splits[8], 1), 0, 1)
    mask_out = with_ends((jax.random.randint(splits[9], (VH * HD // TILE, D // TILE), 0, 4) < 3).astype(jnp.int32), jax.random.fold_in(splits[9], 1), 0, 1)
    decay_rate = draw_decay_rate(jax.random.fold_in(splits[12], 71), 0)
    norm_gain = jnp.clip(1.0 + 0.18 * jax.random.normal(splits[11], (HD,), jnp.float32), 0.1, 1.9)
    return dict(tokens=tokens, w_query=w_query, w_key=w_key, w_value=w_value, w_beta=w_beta, w_out=w_out, mask_query=mask_query, mask_key=mask_key, mask_value=mask_value, mask_out=mask_out, decay_rate=decay_rate, norm_gain=norm_gain)


def masked(weight, mask):
    tall, broad = mask.shape
    full = jnp.broadcast_to(mask[:, None, :, None], (tall, TILE, broad, TILE)).reshape(tall * TILE, broad * TILE)
    return weight * full.astype(weight.dtype)

def unit_rows(matrix):
    return matrix * lax.rsqrt(lax.optimization_barrier(jnp.sum(matrix * matrix, -1, keepdims=True)) + 1e-06)

def projections(tokens, w_query, w_key, w_value, w_beta, mask_query, mask_key, mask_value):
    row_count = tokens.shape[0]
    raw_q = jnp.dot(tokens.astype(jnp.float32), masked(w_query, mask_query).astype(jnp.float32), preferred_element_type=jnp.float32)
    raw_k = jnp.dot(tokens.astype(jnp.float32), masked(w_key, mask_key).astype(jnp.float32), preferred_element_type=jnp.float32)
    raw_v = jnp.dot(tokens.astype(jnp.float32), masked(w_value, mask_value).astype(jnp.float32), preferred_element_type=jnp.float32)
    beta_gate = jax.nn.sigmoid(jnp.dot(tokens.astype(jnp.float32), w_beta.astype(jnp.float32), preferred_element_type=jnp.float32))
    queries = (unit_rows(raw_q.reshape(row_count, -1, HD)) * (1.0 / math.sqrt(HD))).astype(jnp.bfloat16)
    keys = unit_rows(raw_k.reshape(row_count, -1, HD)).astype(jnp.bfloat16)
    values = jax.nn.silu(raw_v.reshape(row_count, -1, HD)).astype(jnp.bfloat16)
    return (queries, keys, values, beta_gate)

def blocks(array):
    return array.reshape(array.shape[0] // BLOCK_LEN, BLOCK_LEN, array.shape[1], -1).transpose(0, 2, 1, 3)

def block_parts(query_pairs, key_pairs, keys, values, beta_gate, decay_rate):
    highest = lax.Precision.HIGHEST
    factor = keys.shape[-3] // key_pairs.shape[-3]
    log_decay = jnp.cumsum(jnp.log(decay_rate), axis=-1)
    spread = log_decay[..., :, None] - log_decay[..., None, :]
    positions = jnp.arange(BLOCK_LEN)
    lower_mask = positions[:, None] >= positions[None, :]
    strict_mask = positions[:, None] > positions[None, :]
    decay_ratio = jnp.where(lower_mask, jnp.exp(jnp.where(lower_mask, spread, 0.0)), 0.0)
    wide_pairs = key_pairs.astype(jnp.float32)
    key_gram = jnp.repeat(jnp.einsum('...id,...jd->...ij', wide_pairs, wide_pairs, precision=highest), factor, axis=-3)
    identity = jnp.eye(BLOCK_LEN, dtype=jnp.float32)
    system = identity + jnp.where(strict_mask, beta_gate[..., :, None] * decay_ratio * key_gram, 0.0)
    right_side = jnp.concatenate([(beta_gate * jnp.exp(log_decay))[..., None] * keys, beta_gate[..., None] * values], -1)
    solved = jax.scipy.linalg.solve_triangular(system, right_side, lower=True, unit_diagonal=True)
    key_mix = solved[..., :HD]
    value_mix = solved[..., HD:]
    pair_scores = jnp.einsum('...id,...jd->...ij', query_pairs.astype(jnp.float32), wide_pairs, precision=highest)
    scores = jnp.repeat(pair_scores, factor, axis=-3) * decay_ratio
    return (log_decay, key_mix, value_mix, scores)

def block_step(carried, inputs):
    highest = lax.Precision.HIGHEST
    queries, keys, log_decay, key_mix, value_mix, scores = inputs
    corrected = value_mix - jnp.einsum('hcd,hdw->hcw', key_mix, carried, precision=highest)
    last_log = log_decay[:, -1]
    tail_decay = jnp.exp(last_log[:, None] - log_decay)
    updated = jnp.exp(last_log)[:, None, None] * carried + jnp.einsum('hcd,hcw->hdw', keys * tail_decay[..., None], corrected, precision=highest)
    emitted = jnp.exp(log_decay)[..., None] * jnp.einsum('hcd,hdw->hcw', queries, carried, precision=highest)
    emitted = emitted + jnp.einsum('hij,hjw->hiw', scores, corrected, precision=highest)
    return (updated, emitted)

def normalize(outputs, norm_gain):
    block_count, head_count, span_len, width = outputs.shape
    flattened = outputs.transpose(0, 2, 1, 3).reshape(block_count * span_len, head_count, width)
    inv_rms = lax.rsqrt(lax.optimization_barrier(jnp.mean(flattened * flattened, -1, keepdims=True)) + 1e-06)
    return (flattened * inv_rms * norm_gain).astype(jnp.bfloat16).reshape(block_count * span_len, head_count * width)

def reference(tokens, w_query, w_key, w_value, w_beta, w_out, mask_query, mask_key, mask_value, mask_out, decay_rate, norm_gain):
    queries, keys, values, beta_gate = projections(tokens, w_query, w_key, w_value, w_beta, mask_query, mask_key, mask_value)
    repeat_factor = VH // KH
    query_pairs = blocks(queries)
    key_pairs = blocks(keys)
    query_blocks = blocks(jnp.repeat(queries, repeat_factor, axis=1).astype(jnp.float32))
    key_blocks = blocks(jnp.repeat(keys, repeat_factor, axis=1).astype(jnp.float32))
    value_blocks = blocks(values.astype(jnp.float32))
    beta_blocks = blocks(beta_gate[..., None])[..., 0]
    decay_blocks = blocks(decay_rate[..., None])[..., 0]

    def advance(carried, inputs):
        pair_q, pair_k, block_q, block_k, block_v, block_b, block_d = inputs
        log_decay, key_mix, value_mix, scores = block_parts(pair_q, pair_k, block_k, block_v, block_b, block_d)
        return block_step(carried, (block_q, block_k, log_decay, key_mix, value_mix, scores))
    initial = jnp.zeros((VH, HD, HD), jnp.float32)
    closing, outputs = lax.scan(advance, initial, (query_pairs, key_pairs, query_blocks, key_blocks, value_blocks, beta_blocks, decay_blocks))
    hidden = normalize(outputs, norm_gain)
    return jnp.dot(hidden.astype(jnp.float32), masked(w_out, mask_out).astype(jnp.float32), preferred_element_type=jnp.float32).astype(jnp.bfloat16)
```

```python
import functools
import math

import jax
import jax.numpy as jnp
from jax import lax
from jax.experimental import pallas as pl
from jax.experimental.pallas import tpu as pltpu
from jax.sharding import PartitionSpec as P

HD = 128
TILE = 64
RING = 8
CORES = 2
MESH = pl.DeviceIdType.MESH
F32 = jnp.float32
BF16 = jnp.bfloat16


def mm(left, right):
    return jnp.dot(left.astype(BF16), right.astype(BF16), preferred_element_type=F32)


def mm_nt(left, right):
    return lax.dot_general(
        left, right, (((1,), (1,)), ((), ())), preferred_element_type=F32
    )


def split(matrix):
    high = matrix.astype(BF16)
    return high, (matrix - high.astype(F32)).astype(BF16)


def mm_split(left, right):
    left_high, left_low = split(left)
    right_high, right_low = split(right)
    return (
        jnp.dot(left_high, right_high, preferred_element_type=F32)
        + jnp.dot(left_high, right_low, preferred_element_type=F32)
        + jnp.dot(left_low, right_high, preferred_element_type=F32)
    )


def unit_rows(matrix):
    return matrix * lax.rsqrt(jnp.sum(matrix * matrix, -1, keepdims=True) + 1e-06)


def spread_blocks(columns, count):
    rows = columns.shape[0]
    first = lax.broadcasted_iota(jnp.int32, (rows, 2 * TILE), 1) < TILE
    return jnp.concatenate(
        [
            jnp.where(first, columns[:, 2 * i : 2 * i + 1], columns[:, 2 * i + 1 : 2 * i + 2])
            for i in range(count // 2)
        ],
        axis=1,
    )


def unit_lower_inverse(lower, row, col):
    size = lower.shape[0]
    inverse = jnp.where(row == col, 1.0, 0.0) - jnp.where((row >> 1) == (col >> 1), lower, 0.0)
    shift = 1
    while (1 << shift) < size:
        corner = ((row >> (shift + 1)) == (col >> (shift + 1))) & ((row >> shift) != (col >> shift))
        inverse = inverse - mm_split(inverse, mm_split(jnp.where(corner, lower, 0.0), inverse))
        shift += 1
    return inverse


def kernel(
    seq_count,
    head_count,
    tokens_ref,
    w_query_ref,
    w_key_ref,
    w_value_ref,
    w_beta_ref,
    w_out_ref,
    mask_query_ref,
    mask_key_ref,
    mask_value_ref,
    mask_out_ref,
    decay_ref,
    gain_ref,
    out_ref,
    w_in,
    w_o,
    tok,
    small,
    rows_in,
    rows_out,
    local_out,
    local_q,
    ab_send,
    ab_recv,
    prefix,
    x_send,
    x_recv,
    s_send,
    s_recv,
    hidden,
    pair_send,
    pair_recv,
    own_part,
    sum_send,
    sum_recv,
    w_sem,
    tok_send_sem,
    tok_recv_sem,
    sib_send_sem,
    sib_recv_sem,
    ab_send_sem,
    ab_recv_sem,
    x_send_sem,
    x_recv_sem,
    s_send_sem,
    s_recv_sem,
    pair_send_sem,
    pair_recv_sem,
    sum_send_sem,
    sum_recv_sem,
):
    s = lax.axis_index("seq")
    hd = lax.axis_index("head")
    chips_x = seq_count // RING
    chips_y = head_count // CORES
    x, z = s // RING, lax.rem(s, RING)
    y, core = hd // CORES, lax.rem(hd, CORES)
    piece, width = tokens_ref.shape
    span = piece * head_count
    key_cols = w_query_ref.shape[1]
    value_cols = w_value_ref.shape[1]
    heads = value_cols // HD
    key_heads = key_cols // HD
    in_cols = 2 * key_cols + value_cols

    weight_copies = [
        pltpu.make_async_copy(w_query_ref, w_in.at[:, pl.ds(0, key_cols)], w_sem.at[0]),
        pltpu.make_async_copy(w_key_ref, w_in.at[:, pl.ds(key_cols, key_cols)], w_sem.at[1]),
        pltpu.make_async_copy(w_value_ref, w_in.at[:, pl.ds(2 * key_cols, value_cols)], w_sem.at[2]),
        pltpu.make_async_copy(w_out_ref, w_o, w_sem.at[3]),
    ]
    for copy in weight_copies:
        copy.start()

    def at_y(step):
        return (s, lax.rem(y + step, chips_y) * CORES + core)

    sibling = (s, y * CORES + (1 - core))

    def at_z(place):
        return (x * RING + place, hd)

    def at_x(step):
        return (lax.rem(x + step, chips_x) * RING + z, hd)

    barrier = pltpu.get_barrier_semaphore()
    partners = [at_y(step) for step in range(1, chips_y)]
    partners += [sibling]
    partners += [at_z(lax.rem(z + step, RING)) for step in range(1, RING)]
    partners += [at_x(step) for step in range(1, chips_x)]
    for partner in partners:
        pl.semaphore_signal(barrier, inc=1, device_id=partner, device_id_type=MESH)
    pl.semaphore_wait(barrier, len(partners))

    def push(source, target, send_sem, recv_sem, device):
        return pltpu.make_async_remote_copy(
            src_ref=source,
            dst_ref=target,
            send_sem=send_sem,
            recv_sem=recv_sem,
            device_id=device,
            device_id_type=MESH,
        )

    far_first = sorted(range(1, chips_y), key=lambda step: -min(step, chips_y - step))
    token_pushes = {
        step: push(
            tokens_ref, tok.at[hd], tok_send_sem.at[step], tok_recv_sem.at[step], at_y(step)
        )
        for step in far_first
    }
    for step in far_first:
        token_pushes[step].start()
    sibling_pushes = [
        push(tokens_ref, tok.at[hd], sib_send_sem.at[0], sib_recv_sem.at[0], sibling)
    ]
    sibling_pushes[0].start()
    tok[hd] = tokens_ref[...]

    small[...] = jnp.zeros_like(small)
    mask_blocks = 0
    for ref in (mask_query_ref, mask_key_ref, mask_value_ref):
        small[mask_blocks : mask_blocks + ref.shape[0], 0 : ref.shape[1]] = ref[...].astype(F32)
        mask_blocks += ref.shape[0]
    turned = jnp.transpose(small[:, 0:HD])
    rows_in[...] = spread_blocks(turned[0 : rows_in.shape[0], :], mask_blocks)
    rows_out[...] = spread_blocks(mask_out_ref[...].astype(F32), mask_out_ref.shape[1])

    for copy in weight_copies[:3]:
        copy.wait()

    def mask_in(i, carry):
        at = pl.ds(pl.multiple_of(i * TILE, TILE), TILE)
        w_in[at, :] = (w_in[at, :].astype(F32) * rows_in[pl.ds(i, 1), :]).astype(BF16)
        return carry

    lax.fori_loop(0, width // TILE, mask_in, 0)

    for step in sorted(range(1, chips_y), key=lambda step: min(step, chips_y - step)):
        token_pushes[step].wait_recv()
        held = tok.at[lax.rem(y + chips_y - step, chips_y) * CORES + core]
        forward = push(held, held, sib_send_sem.at[step], sib_recv_sem.at[step], sibling)
        forward.start()
        sibling_pushes.append(forward)

    weight_copies[3].wait()

    def mask_o(i, carry):
        at = pl.ds(pl.multiple_of(i * TILE, TILE), TILE)
        w_o[at, :] = (w_o[at, :].astype(F32) * rows_out[pl.ds(i, 1), :]).astype(BF16)
        return carry

    lax.fori_loop(0, value_cols // TILE, mask_o, 0)

    row = lax.broadcasted_iota(jnp.int32, (span, span), 0)
    col = lax.broadcasted_iota(jnp.int32, (span, span), 1)
    log_rows = jnp.dot(
        jnp.log(decay_ref[...]),
        jnp.where(row <= col, 1.0, 0.0),
        precision=lax.Precision.HIGHEST,
        preferred_element_type=F32,
    )

    for forward in sibling_pushes:
        forward.wait_recv()

    gathered = tok[...].reshape(span, width)
    beta_rows = jax.nn.sigmoid(mm_nt(w_beta_ref[...], gathered))
    small[0:heads, :] = log_rows
    small[8 : 8 + heads, :] = beta_rows
    columns = jnp.transpose(small[...])

    raw_q = jnp.dot(gathered, w_in[:, 0:key_cols], preferred_element_type=F32)
    raw_k = jnp.dot(gathered, w_in[:, key_cols : 2 * key_cols], preferred_element_type=F32)
    queries, keys, key_turned, grams, pair_scores = [], [], [], [], []
    for i in range(key_heads):
        at = slice(i * HD, (i + 1) * HD)
        query = (unit_rows(raw_q[:, at]) * (1.0 / math.sqrt(HD))).astype(BF16)
        key = unit_rows(raw_k[:, at]).astype(BF16)
        queries.append(query.astype(F32))
        keys.append(key.astype(F32))
        key_turned.append(jnp.transpose(key.astype(F32)))
        grams.append(mm_nt(key, key))
        pair_scores.append(mm_nt(query, key))
    raw_v = jnp.dot(gathered, w_in[:, 2 * key_cols : in_cols], preferred_element_type=F32)
    values = jax.nn.silu(raw_v).astype(BF16).astype(F32)

    eye = jnp.where(
        lax.broadcasted_iota(jnp.int32, (HD, HD), 0) == lax.broadcasted_iota(jnp.int32, (HD, HD), 1),
        1.0,
        0.0,
    )
    is_root = lax.rem(z, CORES) == core
    ab_pushes = []
    for h in range(heads):
        i = h * key_heads // heads
        log_row = log_rows[h : h + 1, :]
        log_col = columns[:, h : h + 1]
        beta_col = columns[:, 8 + h : 9 + h]
        last = log_row[:, span - 1 : span]
        decay = jnp.where(row >= col, jnp.exp(jnp.where(row >= col, log_col - log_row, 0.0)), 0.0)
        lower = jnp.where(row > col, beta_col * decay * grams[i], 0.0)
        inverse = unit_lower_inverse(lower, row, col)
        rise = jnp.exp(log_col)
        value = values[:, h * HD : (h + 1) * HD]
        mixed = mm(
            inverse,
            jnp.concatenate([(beta_col * rise) * keys[i], beta_col * value], axis=1),
        ).astype(BF16)
        tail_keys = key_turned[i] * jnp.exp(last - log_row)
        end = mm(tail_keys, mixed)
        transition = jnp.exp(last) * eye - end[:, 0:HD]
        ab_send[h] = jnp.concatenate([transition, end[:, HD : 2 * HD]], axis=1).astype(BF16)
        target = h * CORES + core
        copy = push(ab_send.at[h], ab_recv.at[z], ab_send_sem.at[h], ab_recv_sem.at[z], at_z(target))
        ab_pushes.append((target, copy))

        @pl.when(z != target)
        def _():
            copy.start()

        @pl.when(z == target)
        def _():
            ab_recv[z] = ab_send[h]

        read = mm(pair_scores[i] * decay, mixed)
        local_out[h] = read[:, HD : 2 * HD]
        local_q[h] = (rise * queries[i] - read[:, 0:HD]).astype(BF16)

    def s_push(place):
        mine = z // CORES
        return push(
            s_send.at[place], s_recv.at[mine], s_send_sem.at[place], s_recv_sem.at[mine], at_z(place)
        )

    def recv_ab(place):
        return push(
            ab_send.at[0], ab_recv.at[place], ab_send_sem.at[0], ab_recv_sem.at[place], at_z(place)
        )

    @pl.when(is_root)
    def _():
        running = None
        for place in range(RING):
            @pl.when(z != place)
            def _():
                recv_ab(place).wait_recv()

            pair = ab_recv[place]
            if place == 0:
                running = pair.astype(F32)
            else:
                running = mm(pair[:, 0:HD], running)
                running = jnp.concatenate(
                    [running[:, 0:HD], running[:, HD : 2 * HD] + pair[:, HD : 2 * HD].astype(F32)], axis=1
                )
            if place < RING - 1:
                prefix[place] = running
        x_send[...] = running.astype(BF16)
        x_pushes = [
            push(x_send, x_recv.at[x], x_send_sem.at[step], x_recv_sem.at[step], at_x(step))
            for step in range(1, chips_x)
        ]
        for copy in x_pushes:
            copy.start()
        x_recv[x] = x_send[...]
        for copy in x_pushes:
            copy.wait_recv()
        state = jnp.zeros((HD, HD), F32)
        for place in range(chips_x - 1):
            pair = x_recv[place]
            after = mm(pair[:, 0:HD], state) + pair[:, HD : 2 * HD].astype(F32)
            state = jnp.where(place < x, after, state)
        for place in range(RING):
            if place == 0:
                start = state
            else:
                start = mm(prefix[place - 1, :, 0:HD], state) + prefix[place - 1, :, HD : 2 * HD]
            s_send[place] = start.astype(BF16)

            @pl.when(z != place)
            def _():
                s_push(place).start()

            @pl.when(z == place)
            def _():
                s_recv[z // CORES] = s_send[place]

        for copy in x_pushes:
            copy.wait_send()
        for place in range(RING):
            @pl.when(z != place)
            def _():
                s_push(place).wait_send()

    for h in range(heads):
        source = h * CORES + core

        @pl.when(z != source)
        def _():
            push(
                s_send.at[0], s_recv.at[h], s_send_sem.at[0], s_recv_sem.at[h], at_z(source)
            ).wait_recv()

        state_out = local_out[h] + jnp.dot(local_q[h], s_recv[h], preferred_element_type=F32)
        inv_rms = lax.rsqrt(jnp.mean(state_out * state_out, -1, keepdims=True) + 1e-06)
        hidden[:, :, h * HD : (h + 1) * HD] = (
            (state_out * inv_rms * gain_ref[...]).astype(BF16).reshape(head_count, piece, HD)
        )

    order = far_first + [0]

    def project(which_core):
        rows = jnp.concatenate(
            [hidden[lax.rem(y + step, chips_y) * CORES + which_core] for step in order], axis=0
        )
        return jnp.dot(rows, w_o[...], preferred_element_type=F32)

    pair_send[...] = project(1 - core).astype(BF16).reshape(chips_y, piece, width)
    pair_pushes = [
        push(pair_send.at[n], pair_recv.at[n], pair_send_sem.at[n], pair_recv_sem.at[n], sibling)
        for n in range(chips_y)
    ]
    for copy in pair_pushes:
        copy.start()
    own_part[...] = project(core).reshape(chips_y, piece, width)
    sum_pushes = []
    for n, step in enumerate(order):
        pair_pushes[n].wait_recv()
        both = own_part[n] + pair_recv[n].astype(F32)
        if step == 0:
            total = both
        else:
            sum_send[n] = both.astype(BF16)
            copy = push(sum_send.at[n], sum_recv.at[n], sum_send_sem.at[n], sum_recv_sem.at[n], at_y(step))
            copy.start()
            sum_pushes.append(copy)
    for n, copy in enumerate(sum_pushes):
        copy.wait_recv()
        total = total + sum_recv[n].astype(F32)
    out_ref[...] = total.astype(BF16)

    for step in far_first:
        token_pushes[step].wait_send()
    for copy in sibling_pushes + pair_pushes + sum_pushes:
        copy.wait_send()
    for target, copy in ab_pushes:
        @pl.when(z != target)
        def _():
            copy.wait_send()


def on_device(
    seq_count,
    head_count,
    tokens,
    w_query,
    w_key,
    w_value,
    w_beta,
    w_out,
    mask_query,
    mask_key,
    mask_value,
    mask_out,
    decay_rate,
    norm_gain,
):
    piece, width = tokens.shape
    span = piece * head_count
    value_cols = w_value.shape[1]
    in_cols = 2 * w_query.shape[1] + value_cols
    heads = value_cols // HD
    chips_x = seq_count // RING
    chips_y = head_count // CORES
    vmem = pl.BlockSpec(memory_space=pltpu.VMEM)
    hbm = pl.BlockSpec(memory_space=pl.ANY)
    dma = pltpu.SemaphoreType.DMA
    return pl.pallas_call(
        functools.partial(kernel, seq_count, head_count),
        out_shape=jax.ShapeDtypeStruct((piece, width), BF16),
        in_specs=[vmem, hbm, hbm, hbm, vmem, hbm] + [vmem] * 6,
        out_specs=vmem,
        scratch_shapes=[
            pltpu.VMEM((width, in_cols), BF16),
            pltpu.VMEM((value_cols, width), BF16),
            pltpu.VMEM((head_count, piece, width), BF16),
            pltpu.VMEM((HD, span), F32),
            pltpu.VMEM((width // TILE, in_cols), F32),
            pltpu.VMEM((value_cols // TILE, width), F32),
            pltpu.VMEM((heads, span, HD), F32),
            pltpu.VMEM((heads, span, HD), BF16),
            pltpu.VMEM((heads, HD, 2 * HD), BF16),
            pltpu.VMEM((RING, HD, 2 * HD), BF16),
            pltpu.VMEM((RING - 1, HD, 2 * HD), F32),
            pltpu.VMEM((HD, 2 * HD), BF16),
            pltpu.VMEM((chips_x, HD, 2 * HD), BF16),
            pltpu.VMEM((RING, HD, HD), BF16),
            pltpu.VMEM((heads, HD, HD), BF16),
            pltpu.VMEM((head_count, piece, value_cols), BF16),
            pltpu.VMEM((chips_y, piece, width), BF16),
            pltpu.VMEM((chips_y, piece, width), BF16),
            pltpu.VMEM((chips_y, piece, width), F32),
            pltpu.VMEM((chips_y - 1, piece, width), BF16),
            pltpu.VMEM((chips_y - 1, piece, width), BF16),
            dma((4,)),
            dma((chips_y,)),
            dma((chips_y,)),
            dma((chips_y,)),
            dma((chips_y,)),
            dma((heads,)),
            dma((RING,)),
            dma((chips_x,)),
            dma((chips_x,)),
            dma((RING,)),
            dma((heads,)),
            dma((chips_y,)),
            dma((chips_y,)),
            dma((chips_y - 1,)),
            dma((chips_y - 1,)),
        ],
        compiler_params=pltpu.CompilerParams(
            collective_id=0, has_side_effects=True, vmem_limit_bytes=48 * 1024 * 1024
        ),
        name="layer",
    )(
        tokens,
        w_query,
        w_key,
        w_value,
        w_beta.T,
        w_out,
        mask_query.T,
        mask_key.T,
        mask_value.T,
        mask_out,
        decay_rate.T,
        norm_gain.reshape(1, HD),
    )


def solution(mesh):
    return jax.shard_map(
        functools.partial(on_device, mesh.shape["seq"], mesh.shape["head"]),
        mesh=mesh,
        in_specs=(
            P(("seq", "head"), None),
            P(None, "head"),
            P(None, "head"),
            P(None, "head"),
            P(None, "head"),
            P("head", None),
            P(None, "head"),
            P(None, "head"),
            P(None, "head"),
            P("head", None),
            P("seq", "head"),
            P(),
        ),
        out_specs=P(("seq", "head"), None),
        check_vma=False,
    )
```

```python
import functools
import math

import jax
import jax.numpy as jnp
from jax import lax
from jax.experimental import pallas as pl
from jax.experimental.pallas import tpu as pltpu
from jax.sharding import PartitionSpec as P

HD = 128
TILE = 64
RING = 8
CORES = 2
GROUPS = 1
MESH = pl.DeviceIdType.MESH
F32 = jnp.float32
BF16 = jnp.bfloat16


def mm(left, right):
    return jnp.dot(left.astype(BF16), right.astype(BF16), preferred_element_type=F32)


def mm_nt(left, right):
    return lax.dot_general(
        left, right, (((1,), (1,)), ((), ())), preferred_element_type=F32
    )


def unit_rows(matrix):
    return matrix * lax.rsqrt(jnp.sum(matrix * matrix, -1, keepdims=True) + 1e-06)


def spread_blocks(columns, count):
    rows = columns.shape[0]
    first = lax.broadcasted_iota(jnp.int32, (rows, 2 * TILE), 1) < TILE
    return jnp.concatenate(
        [
            jnp.where(first, columns[:, 2 * i : 2 * i + 1], columns[:, 2 * i + 1 : 2 * i + 2])
            for i in range(count // 2)
        ],
        axis=1,
    )


def unit_lower_inverses(lowers, row, col):
    size = row.shape[0]
    eye = jnp.where(row == col, 1.0, 0.0)
    pairs = (row >> 1) == (col >> 1)
    negated = [(-lower).astype(BF16) for lower in lowers]
    inverses = [(eye - jnp.where(pairs, lower, 0.0)).astype(BF16) for lower in lowers]
    shift = 1
    while (1 << shift) < size:
        corner = ((row >> (shift + 1)) == (col >> (shift + 1))) & ((row >> shift) != (col >> shift))
        corner = jnp.where(corner, 1.0, 0.0).astype(BF16)
        halves = [mm(inverse, lower * corner).astype(BF16) for inverse, lower in zip(inverses, negated)]
        inverses = [inverse + mm(half, inverse).astype(BF16) for inverse, half in zip(inverses, halves)]
        shift += 1
    return inverses


def kernel(
    seq_count,
    head_count,
    tokens_ref,
    w_query_ref,
    w_key_ref,
    w_value_ref,
    w_beta_hbm,
    w_out_ref,
    mask_query_hbm,
    mask_key_hbm,
    mask_value_hbm,
    mask_out_hbm,
    decay_hbm,
    gain_hbm,
    out_ref,
    w_beta_ref,
    mask_query_ref,
    mask_key_ref,
    mask_value_ref,
    mask_out_ref,
    decay_ref,
    gain_ref,
    w_in,
    w_o,
    tok,
    small,
    rows_in,
    rows_out,
    local_out,
    local_q,
    ab_send,
    ab_recv,
    prefix,
    x_send,
    x_recv,
    s_send,
    s_recv,
    hidden,
    pair_send,
    pair_recv,
    own_part,
    sum_send,
    sum_recv,
    w_sem,
    small_sem,
    tok_send_sem,
    tok_recv_sem,
    sib_send_sem,
    sib_recv_sem,
    ab_send_sem,
    ab_recv_sem,
    x_send_sem,
    x_recv_sem,
    s_send_sem,
    s_recv_sem,
    pair_send_sem,
    pair_recv_sem,
    sum_send_sem,
    sum_recv_sem,
):
    s = lax.axis_index("seq")
    hd = lax.axis_index("head")
    chips_x = seq_count // RING
    chips_y = head_count // CORES
    x, z = s // RING, lax.rem(s, RING)
    y, core = hd // CORES, lax.rem(hd, CORES)
    piece, width = tokens_ref.shape
    span = piece * head_count
    key_cols = w_query_ref.shape[1]
    value_cols = w_value_ref.shape[1]
    heads = value_cols // HD
    key_heads = key_cols // HD
    in_cols = 2 * key_cols + value_cols

    small_copies = [
        pltpu.make_async_copy(source, target, small_sem.at[n])
        for n, (source, target) in enumerate(
            (
                (mask_query_hbm, mask_query_ref),
                (mask_key_hbm, mask_key_ref),
                (mask_value_hbm, mask_value_ref),
                (mask_out_hbm, mask_out_ref),
                (w_beta_hbm, w_beta_ref),
                (decay_hbm, decay_ref),
                (gain_hbm, gain_ref),
                (tokens_ref, tok.at[hd]),
            )
        )
    ]
    for copy in small_copies:
        copy.start()
    weight_copies = [
        pltpu.make_async_copy(w_query_ref, w_in.at[:, pl.ds(0, key_cols)], w_sem.at[0]),
        pltpu.make_async_copy(w_key_ref, w_in.at[:, pl.ds(key_cols, key_cols)], w_sem.at[1]),
        pltpu.make_async_copy(w_value_ref, w_in.at[:, pl.ds(2 * key_cols, value_cols)], w_sem.at[2]),
        pltpu.make_async_copy(w_out_ref, w_o, w_sem.at[3]),
    ]
    for copy in weight_copies:
        copy.start()

    def at_y(step):
        return (s, lax.rem(y + step, chips_y) * CORES + core)

    sibling = (s, y * CORES + (1 - core))

    def at_z(place):
        return (x * RING + place, hd)

    def at_x(step):
        return (lax.rem(x + step, chips_x) * RING + z, hd)

    barrier = pltpu.get_barrier_semaphore()
    partners = [at_y(step) for step in range(1, chips_y)]
    partners += [sibling]
    partners += [at_z(lax.rem(z + step, RING)) for step in range(1, RING)]
    partners += [at_x(step) for step in range(1, chips_x)]
    for partner in partners:
        pl.semaphore_signal(barrier, inc=1, device_id=partner, device_id_type=MESH)
    pl.semaphore_wait(barrier, len(partners))

    def push(source, target, send_sem, recv_sem, device):
        return pltpu.make_async_remote_copy(
            src_ref=source,
            dst_ref=target,
            send_sem=send_sem,
            recv_sem=recv_sem,
            device_id=device,
            device_id_type=MESH,
        )

    far_first = sorted(range(1, chips_y), key=lambda step: -min(step, chips_y - step))
    token_pushes = {
        step: push(
            tokens_ref, tok.at[hd], tok_send_sem.at[step], tok_recv_sem.at[step], at_y(step)
        )
        for step in far_first
    }
    for step in far_first:
        token_pushes[step].start()
    sibling_pushes = [
        push(tokens_ref, tok.at[hd], sib_send_sem.at[0], sib_recv_sem.at[0], sibling)
    ]
    sibling_pushes[0].start()

    for copy in small_copies:
        copy.wait()
    small[...] = jnp.zeros_like(small)
    mask_blocks = 0
    for ref in (mask_query_ref, mask_key_ref, mask_value_ref):
        small[mask_blocks : mask_blocks + ref.shape[0], 0 : ref.shape[1]] = ref[...].astype(F32)
        mask_blocks += ref.shape[0]
    turned = jnp.transpose(small[:, 0:HD])
    rows_in[...] = spread_blocks(turned[0 : rows_in.shape[0], :], mask_blocks)
    rows_out[...] = spread_blocks(mask_out_ref[...].astype(F32), mask_out_ref.shape[1])

    for copy in weight_copies[:3]:
        copy.wait()

    def mask_in(i, carry):
        at = pl.ds(pl.multiple_of(i * TILE, TILE), TILE)
        w_in[at, :] = (w_in[at, :].astype(F32) * rows_in[pl.ds(i, 1), :]).astype(BF16)
        return carry

    lax.fori_loop(0, width // TILE, mask_in, 0)

    for step in sorted(range(1, chips_y), key=lambda step: min(step, chips_y - step)):
        token_pushes[step].wait_recv()
        held = tok.at[lax.rem(y + chips_y - step, chips_y) * CORES + core]
        forward = push(held, held, sib_send_sem.at[step], sib_recv_sem.at[step], sibling)
        forward.start()
        sibling_pushes.append(forward)

    weight_copies[3].wait()

    def mask_o(i, carry):
        at = pl.ds(pl.multiple_of(i * TILE, TILE), TILE)
        w_o[at, :] = (w_o[at, :].astype(F32) * rows_out[pl.ds(i, 1), :]).astype(BF16)
        return carry

    lax.fori_loop(0, value_cols // TILE, mask_o, 0)

    row = lax.broadcasted_iota(jnp.int32, (span, span), 0)
    col = lax.broadcasted_iota(jnp.int32, (span, span), 1)
    log_rows = jnp.dot(
        jnp.log(decay_ref[...]),
        jnp.where(row <= col, 1.0, 0.0),
        precision=lax.Precision.HIGHEST,
        preferred_element_type=F32,
    )

    for forward in sibling_pushes:
        forward.wait_recv()

    gathered = tok[...].reshape(span, width)
    beta_rows = jax.nn.sigmoid(mm_nt(w_beta_ref[...], gathered))
    small[0:heads, :] = log_rows
    small[8 : 8 + heads, :] = beta_rows
    columns = jnp.transpose(small[...])

    raw_q = jnp.dot(gathered, w_in[:, 0:key_cols], preferred_element_type=F32)
    raw_k = jnp.dot(gathered, w_in[:, key_cols : 2 * key_cols], preferred_element_type=F32)
    queries, keys, key_turned, grams, pair_scores = [], [], [], [], []
    for i in range(key_heads):
        at = slice(i * HD, (i + 1) * HD)
        query = (unit_rows(raw_q[:, at]) * (1.0 / math.sqrt(HD))).astype(BF16)
        key = unit_rows(raw_k[:, at]).astype(BF16)
        queries.append(query.astype(F32))
        keys.append(key.astype(F32))
        key_turned.append(jnp.transpose(key.astype(F32)))
        grams.append(mm_nt(key, key))
        pair_scores.append(mm_nt(query, key))
    raw_v = jnp.dot(gathered, w_in[:, 2 * key_cols : in_cols], preferred_element_type=F32)
    values = jax.nn.silu(raw_v).astype(BF16).astype(F32)

    eye = jnp.where(
        lax.broadcasted_iota(jnp.int32, (HD, HD), 0) == lax.broadcasted_iota(jnp.int32, (HD, HD), 1),
        1.0,
        0.0,
    )
    is_root = lax.rem(z, CORES) == core

    def key_head(h):
        return h * key_heads // heads

    ab_pushes = []
    group = heads // GROUPS
    for first_head in range(0, heads, group):
        members = range(first_head, first_head + group)
        lasts = [log_rows[h : h + 1, span - 1 : span] for h in members]
        rises = [jnp.exp(columns[:, h : h + 1]) for h in members]
        betas = [columns[:, 8 + h : 9 + h] for h in members]
        decays = [
            jnp.where(
                row >= col,
                jnp.exp(jnp.where(row >= col, columns[:, h : h + 1] - log_rows[h : h + 1, :], 0.0)),
                0.0,
            )
            for h in members
        ]
        inverses = unit_lower_inverses(
            [
                jnp.where(row > col, beta * decay * grams[key_head(h)], 0.0)
                for h, beta, decay in zip(members, betas, decays)
            ],
            row,
            col,
        )
        mixes = [
            mm(
                inverse,
                jnp.concatenate(
                    [
                        ((beta * rise) * keys[key_head(h)]).astype(BF16),
                        (beta * values[:, h * HD : (h + 1) * HD]).astype(BF16),
                    ],
                    axis=1,
                ),
            ).astype(BF16)
            for h, inverse, beta, rise in zip(members, inverses, betas, rises)
        ]
        ends = [
            mm(key_turned[key_head(h)] * jnp.exp(last - log_rows[h : h + 1, :]), mixed)
            for h, last, mixed in zip(members, lasts, mixes)
        ]
        for h, last, end in zip(members, lasts, ends):
            transition = jnp.exp(last) * eye - end[:, 0:HD]
            ab_send[h] = jnp.concatenate([transition, end[:, HD : 2 * HD]], axis=1).astype(BF16)
            target = h * CORES + core
            copy = push(ab_send.at[h], ab_recv.at[z], ab_send_sem.at[h], ab_recv_sem.at[z], at_z(target))
            ab_pushes.append((target, copy))

            @pl.when(z != target)
            def _():
                copy.start()

            @pl.when(z == target)
            def _():
                ab_recv[z] = ab_send[h]

        reads = [
            mm(pair_scores[key_head(h)] * decay, mixed) for h, decay, mixed in zip(members, decays, mixes)
        ]
        for h, rise, read in zip(members, rises, reads):
            local_out[h] = read[:, HD : 2 * HD]
            local_q[h] = (rise * queries[key_head(h)] - read[:, 0:HD]).astype(BF16)

    def s_push(place):
        mine = z // CORES
        return push(
            s_send.at[place], s_recv.at[mine], s_send_sem.at[place], s_recv_sem.at[mine], at_z(place)
        )

    def recv_ab(place):
        return push(
            ab_send.at[0], ab_recv.at[place], ab_send_sem.at[0], ab_recv_sem.at[place], at_z(place)
        )

    @pl.when(is_root)
    def _():
        running = None
        for place in range(RING):
            @pl.when(z != place)
            def _():
                recv_ab(place).wait_recv()

            pair = ab_recv[place]
            if place == 0:
                running = pair.astype(F32)
            else:
                running = mm(pair[:, 0:HD], running)
                running = jnp.concatenate(
                    [running[:, 0:HD], running[:, HD : 2 * HD] + pair[:, HD : 2 * HD].astype(F32)], axis=1
                )
            if place < RING - 1:
                prefix[place] = running
        x_send[...] = running.astype(BF16)
        x_pushes = [
            push(x_send, x_recv.at[x], x_send_sem.at[step], x_recv_sem.at[step], at_x(step))
            for step in range(1, chips_x)
        ]
        for copy in x_pushes:
            copy.start()
        x_recv[x] = x_send[...]
        for copy in x_pushes:
            copy.wait_recv()
        state = jnp.zeros((HD, HD), F32)
        for place in range(chips_x - 1):
            pair = x_recv[place]
            after = mm(pair[:, 0:HD], state) + pair[:, HD : 2 * HD].astype(F32)
            state = jnp.where(place < x, after, state)
        for place in range(RING):
            if place == 0:
                start = state
            else:
                start = mm(prefix[place - 1, :, 0:HD], state) + prefix[place - 1, :, HD : 2 * HD]
            s_send[place] = start.astype(BF16)

            @pl.when(z != place)
            def _():
                s_push(place).start()

            @pl.when(z == place)
            def _():
                s_recv[z // CORES] = s_send[place]

        for copy in x_pushes:
            copy.wait_send()
        for place in range(RING):
            @pl.when(z != place)
            def _():
                s_push(place).wait_send()

    for h in range(heads):
        source = h * CORES + core

        @pl.when(z != source)
        def _():
            push(
                s_send.at[0], s_recv.at[h], s_send_sem.at[0], s_recv_sem.at[h], at_z(source)
            ).wait_recv()

        state_out = local_out[h] + jnp.dot(local_q[h], s_recv[h], preferred_element_type=F32)
        inv_rms = lax.rsqrt(jnp.mean(state_out * state_out, -1, keepdims=True) + 1e-06)
        hidden[:, :, h * HD : (h + 1) * HD] = (
            (state_out * inv_rms * gain_ref[...]).astype(BF16).reshape(head_count, piece, HD)
        )

    order = far_first + [0]

    def project(which_core):
        rows = jnp.concatenate(
            [hidden[lax.rem(y + step, chips_y) * CORES + which_core] for step in order], axis=0
        )
        return jnp.dot(rows, w_o[...], preferred_element_type=F32)

    pair_send[...] = project(1 - core).astype(BF16).reshape(chips_y, piece, width)
    pair_pushes = [
        push(pair_send.at[n], pair_recv.at[n], pair_send_sem.at[n], pair_recv_sem.at[n], sibling)
        for n in range(chips_y)
    ]
    for copy in pair_pushes:
        copy.start()
    own_part[...] = project(core).reshape(chips_y, piece, width)
    sum_pushes = []
    for n, step in enumerate(order):
        pair_pushes[n].wait_recv()
        both = own_part[n] + pair_recv[n].astype(F32)
        if step == 0:
            total = both
        else:
            sum_send[n] = both.astype(BF16)
            copy = push(sum_send.at[n], sum_recv.at[n], sum_send_sem.at[n], sum_recv_sem.at[n], at_y(step))
            copy.start()
            sum_pushes.append(copy)
    for n, copy in enumerate(sum_pushes):
        copy.wait_recv()
        total = total + sum_recv[n].astype(F32)
    out_ref[...] = total.astype(BF16)

    for step in far_first:
        token_pushes[step].wait_send()
    for copy in sibling_pushes + pair_pushes + sum_pushes:
        copy.wait_send()
    for target, copy in ab_pushes:
        @pl.when(z != target)
        def _():
            copy.wait_send()


def on_device(
    seq_count,
    head_count,
    tokens,
    w_query,
    w_key,
    w_value,
    w_beta,
    w_out,
    mask_query,
    mask_key,
    mask_value,
    mask_out,
    decay_rate,
    norm_gain,
):
    piece, width = tokens.shape
    span = piece * head_count
    value_cols = w_value.shape[1]
    in_cols = 2 * w_query.shape[1] + value_cols
    heads = value_cols // HD
    chips_x = seq_count // RING
    chips_y = head_count // CORES
    vmem = pl.BlockSpec(memory_space=pltpu.VMEM)
    hbm = pl.BlockSpec(memory_space=pltpu.HBM)
    dma = pltpu.SemaphoreType.DMA
    return pl.pallas_call(
        functools.partial(kernel, seq_count, head_count),
        out_shape=jax.ShapeDtypeStruct((piece, width), BF16),
        in_specs=[hbm] * 12,
        out_specs=vmem,
        scratch_shapes=[
            pltpu.VMEM((heads, width), BF16),
            pltpu.VMEM(mask_query.shape[::-1], jnp.int32),
            pltpu.VMEM(mask_key.shape[::-1], jnp.int32),
            pltpu.VMEM(mask_value.shape[::-1], jnp.int32),
            pltpu.VMEM(mask_out.shape, jnp.int32),
            pltpu.VMEM((heads, span), F32),
            pltpu.VMEM((1, HD), F32),
            pltpu.VMEM((width, in_cols), BF16),
            pltpu.VMEM((value_cols, width), BF16),
            pltpu.VMEM((head_count, piece, width), BF16),
            pltpu.VMEM((HD, span), F32),
            pltpu.VMEM((width // TILE, in_cols), F32),
            pltpu.VMEM((value_cols // TILE, width), F32),
            pltpu.VMEM((heads, span, HD), F32),
            pltpu.VMEM((heads, span, HD), BF16),
            pltpu.VMEM((heads, HD, 2 * HD), BF16),
            pltpu.VMEM((RING, HD, 2 * HD), BF16),
            pltpu.VMEM((RING - 1, HD, 2 * HD), F32),
            pltpu.VMEM((HD, 2 * HD), BF16),
            pltpu.VMEM((chips_x, HD, 2 * HD), BF16),
            pltpu.VMEM((RING, HD, HD), BF16),
            pltpu.VMEM((heads, HD, HD), BF16),
            pltpu.VMEM((head_count, piece, value_cols), BF16),
            pltpu.VMEM((chips_y, piece, width), BF16),
            pltpu.VMEM((chips_y, piece, width), BF16),
            pltpu.VMEM((chips_y, piece, width), F32),
            pltpu.VMEM((chips_y - 1, piece, width), BF16),
            pltpu.VMEM((chips_y - 1, piece, width), BF16),
            dma((4,)),
            dma((8,)),
            dma((chips_y,)),
            dma((chips_y,)),
            dma((chips_y,)),
            dma((chips_y,)),
            dma((heads,)),
            dma((RING,)),
            dma((chips_x,)),
            dma((chips_x,)),
            dma((RING,)),
            dma((heads,)),
            dma((chips_y,)),
            dma((chips_y,)),
            dma((chips_y - 1,)),
            dma((chips_y - 1,)),
        ],
        compiler_params=pltpu.CompilerParams(
            collective_id=0, has_side_effects=True, vmem_limit_bytes=60 * 1024 * 1024
        ),
        name="layer",
    )(
        tokens,
        w_query,
        w_key,
        w_value,
        w_beta.T,
        w_out,
        mask_query.T,
        mask_key.T,
        mask_value.T,
        mask_out,
        decay_rate.T,
        norm_gain.reshape(1, HD),
    )


def solution(mesh):
    return jax.shard_map(
        functools.partial(on_device, mesh.shape["seq"], mesh.shape["head"]),
        mesh=mesh,
        in_specs=(
            P(("seq", "head"), None),
            P(None, "head"),
            P(None, "head"),
            P(None, "head"),
            P(None, "head"),
            P("head", None),
            P(None, "head"),
            P(None, "head"),
            P(None, "head"),
            P("head", None),
            P("seq", "head"),
            P(),
        ),
        out_specs=P(("seq", "head"), None),
        check_vma=False,
    )
```

```python
import functools
import math

import jax
import jax.numpy as jnp
from jax import lax
from jax.experimental import pallas as pl
from jax.experimental.pallas import tpu as pltpu
from jax.sharding import PartitionSpec as P

HD = 128
TILE = 64
RING = 8
CORES = 2
MESH = pl.DeviceIdType.MESH
F32 = jnp.float32
BF16 = jnp.bfloat16


def mm(left, right):
    return jnp.dot(left.astype(BF16), right.astype(BF16), preferred_element_type=F32)


def mm_nt(left, right):
    return lax.dot_general(
        left, right, (((1,), (1,)), ((), ())), preferred_element_type=F32
    )


def unit_rows(matrix):
    return matrix * lax.rsqrt(jnp.sum(matrix * matrix, -1, keepdims=True) + 1e-06)


def spread_blocks(columns, count):
    rows = columns.shape[0]
    first = lax.broadcasted_iota(jnp.int32, (rows, 2 * TILE), 1) < TILE
    return jnp.concatenate(
        [
            jnp.where(first, columns[:, 2 * i : 2 * i + 1], columns[:, 2 * i + 1 : 2 * i + 2])
            for i in range(count // 2)
        ],
        axis=1,
    )


def unit_lower_inverses(lowers, row, col):
    size = row.shape[0]
    eye = jnp.where(row == col, 1.0, 0.0)
    pairs = (row >> 1) == (col >> 1)
    negated = [(-lower).astype(BF16) for lower in lowers]
    inverses = [(eye - jnp.where(pairs, lower, 0.0)).astype(BF16) for lower in lowers]
    shift = 1
    while (1 << shift) < size:
        corner = ((row >> (shift + 1)) == (col >> (shift + 1))) & ((row >> shift) != (col >> shift))
        corner = jnp.where(corner, 1.0, 0.0).astype(BF16)
        halves = [mm(inverse, lower * corner).astype(BF16) for inverse, lower in zip(inverses, negated)]
        inverses = [inverse + mm(half, inverse).astype(BF16) for inverse, half in zip(inverses, halves)]
        shift += 1
    return inverses


def kernel(
    seq_count,
    head_count,
    tokens_ref,
    w_query_ref,
    w_key_ref,
    w_value_ref,
    w_beta_hbm,
    w_out_ref,
    mask_query_hbm,
    mask_key_hbm,
    mask_value_hbm,
    mask_out_hbm,
    decay_hbm,
    gain_hbm,
    out_ref,
    w_beta_ref,
    mask_query_ref,
    mask_key_ref,
    mask_value_ref,
    mask_out_ref,
    decay_ref,
    gain_ref,
    w_in,
    w_o,
    w_o_other,
    tok,
    qkv,
    beta_out,
    small,
    rows_in,
    rows_out,
    local_out,
    local_q,
    ab_send,
    ab_recv,
    x_send,
    x_recv,
    s_send,
    s_recv,
    hidden,
    hidden_other,
    own_part,
    sum_send,
    sum_recv,
    w_sem,
    small_sem,
    tok_send_sem,
    tok_recv_sem,
    sib_send_sem,
    sib_recv_sem,
    ab_send_sem,
    ab_recv_sem,
    x_send_sem,
    x_recv_sem,
    s_send_sem,
    s_recv_sem,
    other_send_sem,
    other_recv_sem,
    sum_send_sem,
    sum_recv_sem,
):
    s = lax.axis_index("seq")
    hd = lax.axis_index("head")
    chips_x = seq_count // RING
    chips_y = head_count // CORES
    x, z = s // RING, lax.rem(s, RING)
    y, core = hd // CORES, lax.rem(hd, CORES)
    piece, width = tokens_ref.shape
    span = piece * head_count
    key_cols = w_query_ref.shape[1]
    value_cols = w_value_ref.shape[1]
    heads = value_cols // HD
    key_heads = key_cols // HD
    in_cols = 2 * key_cols + value_cols

    def at_y(step):
        return (s, lax.rem(y + step, chips_y) * CORES + core)

    sibling = (s, y * CORES + (1 - core))

    def at_z(place):
        return (x * RING + place, hd)

    def at_x(step):
        return (lax.rem(x + step, chips_x) * RING + z, hd)

    barrier = pltpu.get_barrier_semaphore()
    partners = [at_y(step) for step in range(1, chips_y)]
    partners += [sibling]
    partners += [at_z(lax.rem(z + step, RING)) for step in range(1, RING)]
    partners += [at_x(step) for step in range(1, chips_x)]
    for partner in partners:
        pl.semaphore_signal(barrier, inc=1, device_id=partner, device_id_type=MESH)
    small_copies = [
        pltpu.make_async_copy(source, target, small_sem.at[n])
        for n, (source, target) in enumerate(
            (
                (mask_query_hbm, mask_query_ref),
                (mask_key_hbm, mask_key_ref),
                (mask_value_hbm, mask_value_ref),
                (mask_out_hbm, mask_out_ref),
                (w_beta_hbm, w_beta_ref),
                (decay_hbm, decay_ref),
                (gain_hbm, gain_ref),
                (tokens_ref, tok.at[hd]),
            )
        )
    ]
    for copy in small_copies:
        copy.start()
    weight_copies = [
        pltpu.make_async_copy(w_query_ref, w_in.at[:, pl.ds(0, key_cols)], w_sem.at[0]),
        pltpu.make_async_copy(w_key_ref, w_in.at[:, pl.ds(key_cols, key_cols)], w_sem.at[1]),
        pltpu.make_async_copy(w_value_ref, w_in.at[:, pl.ds(2 * key_cols, value_cols)], w_sem.at[2]),
        pltpu.make_async_copy(w_out_ref, w_o, w_sem.at[3]),
    ]
    for copy in weight_copies:
        copy.start()
    pl.semaphore_wait(barrier, len(partners))

    def push(source, target, send_sem, recv_sem, device):
        return pltpu.make_async_remote_copy(
            src_ref=source,
            dst_ref=target,
            send_sem=send_sem,
            recv_sem=recv_sem,
            device_id=device,
            device_id_type=MESH,
        )

    far_first = sorted(range(1, chips_y), key=lambda step: -min(step, chips_y - step))
    far_first_x = sorted(range(1, chips_x), key=lambda step: -min(step, chips_x - step))
    token_pushes = {
        step: push(
            tokens_ref, tok.at[hd], tok_send_sem.at[step], tok_recv_sem.at[step], at_y(step)
        )
        for step in far_first
    }
    for step in reversed(far_first):
        token_pushes[step].start()
    sibling_pushes = {
        0: push(tokens_ref, tok.at[hd], sib_send_sem.at[0], sib_recv_sem.at[0], sibling)
    }
    sibling_pushes[0].start()

    for copy in small_copies:
        copy.wait()
    small[...] = jnp.zeros_like(small)
    mask_blocks = 0
    for ref in (mask_query_ref, mask_key_ref, mask_value_ref):
        small[mask_blocks : mask_blocks + ref.shape[0], 0 : ref.shape[1]] = ref[...].astype(F32)
        mask_blocks += ref.shape[0]
    turned = jnp.transpose(small[:, 0:HD])
    rows_in[...] = spread_blocks(turned[0 : rows_in.shape[0], :], mask_blocks)
    rows_out[...] = spread_blocks(mask_out_ref[...].astype(F32), mask_out_ref.shape[1])

    def mask_tiles(weight, rows):
        def step(i, carry):
            at = pl.ds(pl.multiple_of(i * TILE, TILE), TILE)
            kept = jnp.broadcast_to(rows[pl.ds(i, 1), :], (16, rows.shape[1])).astype(BF16)
            tile = weight[at, :].reshape(TILE // 16, 16, rows.shape[1])
            weight[at, :] = (tile * kept[None]).reshape(TILE, rows.shape[1])
            return carry

        lax.fori_loop(0, rows.shape[0], step, 0)

    for copy in weight_copies[:3]:
        copy.wait()
    mask_tiles(w_in, rows_in)
    weight_copies[3].wait()
    mask_tiles(w_o, rows_out)

    row = lax.broadcasted_iota(jnp.int32, (span, span), 0)
    col = lax.broadcasted_iota(jnp.int32, (span, span), 1)
    log_rows = jnp.dot(
        jnp.log(decay_ref[...]),
        jnp.where(row <= col, 1.0, 0.0),
        precision=lax.Precision.HIGHEST,
        preferred_element_type=F32,
    )
    small[0:heads, :] = log_rows
    columns = jnp.transpose(small[...])

    def forward(step):
        token_pushes[step].wait_recv()
        held = tok.at[lax.rem(y + chips_y - step, chips_y) * CORES + core]
        copy = push(held, held, sib_send_sem.at[step], sib_recv_sem.at[step], sibling)
        copy.start()
        sibling_pushes[step] = copy

    def project_in(steps):
        slots = [
            lax.rem(y + chips_y - step, chips_y) * CORES + which for step in steps for which in range(CORES)
        ]
        rows = jnp.concatenate([tok[slot] for slot in slots], axis=0)
        raw = jnp.dot(rows, w_in[...], preferred_element_type=F32)
        beta = jax.nn.sigmoid(mm_nt(rows, w_beta_ref[...]))
        parts = []
        for i in range(key_heads):
            query = unit_rows(raw[:, i * HD : (i + 1) * HD])
            parts.append((query * (1.0 / math.sqrt(HD))).astype(BF16))
        for i in range(key_heads):
            parts.append(unit_rows(raw[:, key_cols + i * HD : key_cols + (i + 1) * HD]).astype(BF16))
        parts.append(jax.nn.silu(raw[:, 2 * key_cols : in_cols]).astype(BF16))
        made = jnp.concatenate(parts, axis=1)
        for n, slot in enumerate(slots):
            qkv[slot] = made[n * piece : (n + 1) * piece]
            beta_out[slot] = beta[n * piece : (n + 1) * piece]

    near = [step for step in far_first if min(step, chips_y - step) == 1]
    far = [step for step in far_first if min(step, chips_y - step) > 1]
    for step in near + far:
        forward(step)
    for step in [0] + near:
        sibling_pushes[step].wait_recv()
    project_in([0] + near)
    if far:
        for step in far:
            sibling_pushes[step].wait_recv()
        project_in(far)

    made = qkv[...].reshape(span, in_cols)
    beta_cols = beta_out[...].reshape(span, heads)
    queries, keys, key_turned, grams, pair_scores = [], [], [], [], []
    for i in range(key_heads):
        query = made[:, i * HD : (i + 1) * HD]
        key = made[:, key_cols + i * HD : key_cols + (i + 1) * HD]
        queries.append(query.astype(F32))
        keys.append(key.astype(F32))
        key_turned.append(jnp.transpose(key.astype(F32)))
        grams.append(mm_nt(key, key))
        pair_scores.append(mm_nt(query, key))
    values = made[:, 2 * key_cols : in_cols].astype(F32)

    eye = jnp.where(
        lax.broadcasted_iota(jnp.int32, (HD, HD), 0) == lax.broadcasted_iota(jnp.int32, (HD, HD), 1),
        1.0,
        0.0,
    )
    is_root = lax.rem(z, CORES) == core

    def key_head(h):
        return h * key_heads // heads

    ab_pushes = []
    far_first_heads = sorted(range(heads), key=lambda turn: -min(turn, heads - turn))
    members = range(heads)
    lasts = [log_rows[h : h + 1, span - 1 : span] for h in members]
    rises = [jnp.exp(columns[:, h : h + 1]) for h in members]
    betas = [beta_cols[:, h : h + 1] for h in members]
    decays = [
        jnp.where(
            row >= col,
            jnp.exp(jnp.where(row >= col, columns[:, h : h + 1] - log_rows[h : h + 1, :], 0.0)),
            0.0,
        )
        for h in members
    ]
    inverses = unit_lower_inverses(
        [
            jnp.where(row > col, beta * decay * grams[key_head(h)], 0.0)
            for h, beta, decay in zip(members, betas, decays)
        ],
        row,
        col,
    )
    mixes = [
        mm(
            inverse,
            jnp.concatenate(
                [
                    ((beta * rise) * keys[key_head(h)]).astype(BF16),
                    (beta * values[:, h * HD : (h + 1) * HD]).astype(BF16),
                ],
                axis=1,
            ),
        ).astype(BF16)
        for h, inverse, beta, rise in zip(members, inverses, betas, rises)
    ]
    ends = [
        mm(key_turned[key_head(h)] * jnp.exp(last - log_rows[h : h + 1, :]), mixed)
        for h, last, mixed in zip(members, lasts, mixes)
    ]
    for h, last, end in zip(members, lasts, ends):
        transition = jnp.exp(last) * eye - end[:, 0:HD]
        ab_send[h] = jnp.concatenate([transition, end[:, HD : 2 * HD]], axis=1).astype(BF16)

    for turn in far_first_heads:
        h = lax.rem(z // CORES + turn, heads)
        target = h * CORES + core
        copy = push(ab_send.at[h], ab_recv.at[z], ab_send_sem.at[turn], ab_recv_sem.at[z], at_z(target))
        ab_pushes.append((turn, copy))
        if turn:
            copy.start()
        else:
            pl.when(jnp.logical_not(is_root))(copy.start)

    @pl.when(is_root)
    def _():
        ab_recv[z] = ab_send[z // CORES]

    w_o_push = push(w_o, w_o_other, other_send_sem.at[0], other_recv_sem.at[0], sibling)
    w_o_push.start()

    reads = [
        mm(pair_scores[key_head(h)] * decay, mixed) for h, decay, mixed in zip(members, decays, mixes)
    ]
    for h, rise, read in zip(members, rises, reads):
        local_out[h] = read[:, HD : 2 * HD]
        local_q[h] = (rise * queries[key_head(h)] - read[:, 0:HD]).astype(BF16)

    def ring_step(step):
        return lax.rem(z + step, RING)

    def s_push(step):
        mine, place = z // CORES, ring_step(step)
        return push(
            s_send.at[place], s_recv.at[mine], s_send_sem.at[step], s_recv_sem.at[mine], at_z(place)
        )

    def after(later, earlier):
        both = mm(later[:, 0:HD], earlier)
        return jnp.concatenate(
            [both[:, 0:HD], both[:, HD : 2 * HD] + later[:, HD : 2 * HD].astype(F32)], axis=1
        )

    def advance(pair, state):
        return mm(pair[:, 0:HD], state) + pair[:, HD : 2 * HD].astype(F32)

    far_first_z = sorted(range(1, RING), key=lambda step: -min(step, RING - step))

    @pl.when(is_root)
    def _():
        for step in reversed(far_first_z):
            place = ring_step(step)
            push(
                ab_send.at[0], ab_recv.at[place], ab_send_sem.at[0], ab_recv_sem.at[place], at_z(place)
            ).wait_recv()
        pairs = [ab_recv[place] for place in range(RING)]
        level = {(place, place + 1): pairs[place] for place in range(RING)}
        size = 1
        while size < RING:
            for low in range(0, RING, 2 * size):
                level[low, low + 2 * size] = after(
                    level[low + size, low + 2 * size], level[low, low + size]
                ).astype(BF16)
            size *= 2
        x_send[...] = level[0, RING]
        x_pushes = [
            push(x_send, x_recv.at[x], x_send_sem.at[step], x_recv_sem.at[step], at_x(step))
            for step in far_first_x
        ]
        for copy in x_pushes:
            copy.start()
        x_recv[x] = x_send[...]
        prefixes = []
        for end in range(1, RING):
            low, total = 0, None
            for size in (4, 2, 1):
                if end & size:
                    part = level[low, low + size]
                    total = part if total is None else after(part, total).astype(BF16)
                    low += size
            prefixes.append(total)
        for copy in x_pushes:
            copy.wait_recv()
        state = jnp.where(x > 0, x_recv[0, :, HD : 2 * HD].astype(F32), 0.0)
        for place in range(1, chips_x - 1):
            state = jnp.where(place < x, advance(x_recv[place], state), state)
        s_send[0] = state.astype(BF16)
        for place in range(1, RING):
            s_send[place] = advance(prefixes[place - 1], state).astype(BF16)
        for step in far_first_z:
            s_push(step).start()
        s_recv[z // CORES] = s_send[z]
        for copy in x_pushes:
            copy.wait_send()
        for step in far_first_z:
            s_push(step).wait_send()

    for h in range(heads):
        source = h * CORES + core

        @pl.when(z != source)
        def _():
            push(
                s_send.at[0], s_recv.at[h], s_send_sem.at[0], s_recv_sem.at[h], at_z(source)
            ).wait_recv()

        state_out = local_out[h] + jnp.dot(local_q[h], s_recv[h], preferred_element_type=F32)
        inv_rms = lax.rsqrt(jnp.mean(state_out * state_out, -1, keepdims=True) + 1e-06)
        hidden[:, :, :, h * HD : (h + 1) * HD] = (
            (state_out * inv_rms * gain_ref[...]).astype(BF16).reshape(chips_y, CORES, piece, HD)
        )

    hidden_push = push(
        hidden.at[:, 1 - core], hidden_other, other_send_sem.at[1], other_recv_sem.at[1], sibling
    )
    hidden_push.start()
    order = far_first + [0]
    places = [lax.rem(y + step, chips_y) for step in order]
    own_rows = jnp.concatenate([hidden[place, core] for place in places], axis=0)
    own_part[...] = jnp.dot(own_rows, w_o[...], preferred_element_type=F32).reshape(chips_y, piece, width)
    w_o_push.wait_recv()
    hidden_push.wait_recv()
    sum_pushes = []
    half = max(chips_y // 2, 1)
    for first in range(0, chips_y, half):
        members = range(first, first + half)
        rows = jnp.concatenate([hidden_other[places[n]] for n in members], axis=0)
        both = jnp.dot(rows, w_o_other[...], preferred_element_type=F32).reshape(half, piece, width)
        both = both + own_part[first : first + half]
        for n in members:
            if order[n] == 0:
                total = both[n - first]
            else:
                sum_send[n] = both[n - first].astype(BF16)
                copy = push(
                    sum_send.at[n], sum_recv.at[n], sum_send_sem.at[n], sum_recv_sem.at[n], at_y(order[n])
                )
                copy.start()
                sum_pushes.append(copy)
    for n, copy in enumerate(sum_pushes):
        copy.wait_recv()
        total = total + sum_recv[n].astype(F32)
    out_ref[...] = total.astype(BF16)

    for step in far_first:
        token_pushes[step].wait_send()
    for copy in list(sibling_pushes.values()) + sum_pushes + [w_o_push, hidden_push]:
        copy.wait_send()
    for turn, copy in ab_pushes:
        if turn:
            copy.wait_send()
        else:
            pl.when(jnp.logical_not(is_root))(copy.wait_send)


def on_device(
    seq_count,
    head_count,
    tokens,
    w_query,
    w_key,
    w_value,
    w_beta,
    w_out,
    mask_query,
    mask_key,
    mask_value,
    mask_out,
    decay_rate,
    norm_gain,
):
    piece, width = tokens.shape
    span = piece * head_count
    value_cols = w_value.shape[1]
    in_cols = 2 * w_query.shape[1] + value_cols
    heads = value_cols // HD
    chips_x = seq_count // RING
    chips_y = head_count // CORES
    vmem = pl.BlockSpec(memory_space=pltpu.VMEM)
    hbm = pl.BlockSpec(memory_space=pltpu.HBM)
    dma = pltpu.SemaphoreType.DMA
    return pl.pallas_call(
        functools.partial(kernel, seq_count, head_count),
        out_shape=pltpu.VMEM((piece, width), BF16),
        in_specs=[hbm] * 12,
        out_specs=vmem,
        scratch_shapes=[
            pltpu.VMEM((heads, width), BF16),
            pltpu.VMEM(mask_query.shape[::-1], jnp.int32),
            pltpu.VMEM(mask_key.shape[::-1], jnp.int32),
            pltpu.VMEM(mask_value.shape[::-1], jnp.int32),
            pltpu.VMEM(mask_out.shape, jnp.int32),
            pltpu.VMEM((heads, span), F32),
            pltpu.VMEM((1, HD), F32),
            pltpu.VMEM((width, in_cols), BF16),
            pltpu.VMEM((value_cols, width), BF16),
            pltpu.VMEM((value_cols, width), BF16),
            pltpu.VMEM((head_count, piece, width), BF16),
            pltpu.VMEM((head_count, piece, in_cols), BF16),
            pltpu.VMEM((head_count, piece, heads), F32),
            pltpu.VMEM((HD, span), F32),
            pltpu.VMEM((width // TILE, in_cols), F32),
            pltpu.VMEM((value_cols // TILE, width), F32),
            pltpu.VMEM((heads, span, HD), F32),
            pltpu.VMEM((heads, span, HD), BF16),
            pltpu.VMEM((heads, HD, 2 * HD), BF16),
            pltpu.VMEM((RING, HD, 2 * HD), BF16),
            pltpu.VMEM((HD, 2 * HD), BF16),
            pltpu.VMEM((chips_x, HD, 2 * HD), BF16),
            pltpu.VMEM((RING, HD, HD), BF16),
            pltpu.VMEM((heads, HD, HD), BF16),
            pltpu.VMEM((chips_y, CORES, piece, value_cols), BF16),
            pltpu.VMEM((chips_y, piece, value_cols), BF16),
            pltpu.VMEM((chips_y, piece, width), F32),
            pltpu.VMEM((chips_y - 1, piece, width), BF16),
            pltpu.VMEM((chips_y - 1, piece, width), BF16),
            dma((4,)),
            dma((8,)),
            dma((chips_y,)),
            dma((chips_y,)),
            dma((chips_y,)),
            dma((chips_y,)),
            dma((heads,)),
            dma((RING,)),
            dma((chips_x,)),
            dma((chips_x,)),
            dma((RING,)),
            dma((heads,)),
            dma((2,)),
            dma((2,)),
            dma((chips_y - 1,)),
            dma((chips_y - 1,)),
        ],
        compiler_params=pltpu.CompilerParams(
            collective_id=0, has_side_effects=True, vmem_limit_bytes=60 * 1024 * 1024
        ),
        name="layer",
    )(
        tokens,
        w_query,
        w_key,
        w_value,
        w_beta.T,
        w_out,
        mask_query.T,
        mask_key.T,
        mask_value.T,
        mask_out,
        decay_rate.T,
        norm_gain.reshape(1, HD),
    )


def solution(mesh):
    return jax.shard_map(
        functools.partial(on_device, mesh.shape["seq"], mesh.shape["head"]),
        mesh=mesh,
        in_specs=(
            P(("seq", "head"), None),
            P(None, "head"),
            P(None, "head"),
            P(None, "head"),
            P(None, "head"),
            P("head", None),
            P(None, "head"),
            P(None, "head"),
            P(None, "head"),
            P("head", None),
            P("seq", "head"),
            P(),
        ),
        out_specs=P(("seq", "head"), None),
        check_vma=False,
    )
```

```python
import functools
import math

import jax
import jax.numpy as jnp
from jax import lax
from jax.experimental import pallas as pl
from jax.experimental.pallas import tpu as pltpu
from jax.sharding import PartitionSpec as P

HD = 128
TILE = 64
RING = 8
CORES = 2
MESH = pl.DeviceIdType.MESH
F32 = jnp.float32
BF16 = jnp.bfloat16


def mm(left, right):
    return jnp.dot(left.astype(BF16), right.astype(BF16), preferred_element_type=F32)


def mm_nt(left, right):
    return lax.dot_general(
        left, right, (((1,), (1,)), ((), ())), preferred_element_type=F32
    )


def unit_rows(matrix):
    return matrix * lax.rsqrt(jnp.sum(matrix * matrix, -1, keepdims=True) + 1e-06)


def spread_blocks(columns, count):
    rows = columns.shape[0]
    first = lax.broadcasted_iota(jnp.int32, (rows, 2 * TILE), 1) < TILE
    return jnp.concatenate(
        [
            jnp.where(first, columns[:, 2 * i : 2 * i + 1], columns[:, 2 * i + 1 : 2 * i + 2])
            for i in range(count // 2)
        ],
        axis=1,
    )


def unit_lower_inverses(lowers, row, col):
    size = row.shape[0]
    eye = jnp.where(row == col, 1.0, 0.0)
    pairs = (row >> 1) == (col >> 1)
    negated = [(-lower).astype(BF16) for lower in lowers]
    inverses = [(eye - jnp.where(pairs, lower, 0.0)).astype(BF16) for lower in lowers]
    shift = 1
    while (1 << shift) < size:
        corner = ((row >> (shift + 1)) == (col >> (shift + 1))) & ((row >> shift) != (col >> shift))
        corner = jnp.where(corner, 1.0, 0.0).astype(BF16)
        halves = [mm(inverse, lower * corner).astype(BF16) for inverse, lower in zip(inverses, negated)]
        inverses = [inverse + mm(half, inverse).astype(BF16) for inverse, half in zip(inverses, halves)]
        shift += 1
    return inverses


def push(source, target, send_sem, recv_sem, device):
    return pltpu.make_async_remote_copy(
        src_ref=source,
        dst_ref=target,
        send_sem=send_sem,
        recv_sem=recv_sem,
        device_id=device,
        device_id_type=MESH,
    )


def greet(partners):
    barrier = pltpu.get_barrier_semaphore()
    for partner in partners:
        pl.semaphore_signal(barrier, inc=1, device_id=partner, device_id_type=MESH)
    return lambda: pl.semaphore_wait(barrier, len(partners))


def far_first_steps(count):
    return sorted(range(1, count), key=lambda step: -min(step, count - step))


def gather_kernel(
    head_count,
    tokens_ref,
    w_query_ref,
    w_key_ref,
    w_value_ref,
    w_beta_hbm,
    w_out_ref,
    mask_query_hbm,
    mask_key_hbm,
    mask_value_hbm,
    mask_out_hbm,
    decay_hbm,
    qkv,
    beta_out,
    w_o,
    log_rows_ref,
    columns_ref,
    w_beta_ref,
    mask_query_ref,
    mask_key_ref,
    mask_value_ref,
    mask_out_ref,
    decay_ref,
    w_in,
    tok,
    small,
    rows_in,
    rows_out,
    w_sem,
    small_sem,
    tok_send_sem,
    tok_recv_sem,
    sib_send_sem,
    sib_recv_sem,
):
    s = lax.axis_index("seq")
    hd = lax.axis_index("head")
    chips_y = head_count // CORES
    y, core = hd // CORES, lax.rem(hd, CORES)
    piece, width = tokens_ref.shape
    span = piece * head_count
    key_cols = w_query_ref.shape[1]
    value_cols = w_value_ref.shape[1]
    heads = value_cols // HD
    key_heads = key_cols // HD
    in_cols = 2 * key_cols + value_cols

    def at_y(step):
        return (s, lax.rem(y + step, chips_y) * CORES + core)

    sibling = (s, y * CORES + (1 - core))
    far_first = far_first_steps(chips_y)
    wait_partners = greet([at_y(step) for step in range(1, chips_y)] + [sibling])

    small_copies = [
        pltpu.make_async_copy(source, target, small_sem.at[n])
        for n, (source, target) in enumerate(
            (
                (mask_query_hbm, mask_query_ref),
                (mask_key_hbm, mask_key_ref),
                (mask_value_hbm, mask_value_ref),
                (mask_out_hbm, mask_out_ref),
                (w_beta_hbm, w_beta_ref),
                (decay_hbm, decay_ref),
                (tokens_ref, tok.at[hd]),
            )
        )
    ]
    for copy in small_copies:
        copy.start()
    weight_copies = [
        pltpu.make_async_copy(w_query_ref, w_in.at[:, pl.ds(0, key_cols)], w_sem.at[0]),
        pltpu.make_async_copy(w_key_ref, w_in.at[:, pl.ds(key_cols, key_cols)], w_sem.at[1]),
        pltpu.make_async_copy(w_value_ref, w_in.at[:, pl.ds(2 * key_cols, value_cols)], w_sem.at[2]),
        pltpu.make_async_copy(w_out_ref, w_o, w_sem.at[3]),
    ]
    for copy in weight_copies:
        copy.start()
    wait_partners()

    token_pushes = {
        step: push(
            tokens_ref, tok.at[hd], tok_send_sem.at[step], tok_recv_sem.at[step], at_y(step)
        )
        for step in far_first
    }
    for step in reversed(far_first):
        token_pushes[step].start()
    sibling_pushes = {
        0: push(tokens_ref, tok.at[hd], sib_send_sem.at[0], sib_recv_sem.at[0], sibling)
    }
    sibling_pushes[0].start()

    for copy in small_copies:
        copy.wait()
    small[...] = jnp.zeros_like(small)
    mask_blocks = 0
    for ref in (mask_query_ref, mask_key_ref, mask_value_ref):
        small[mask_blocks : mask_blocks + ref.shape[0], 0 : ref.shape[1]] = ref[...].astype(F32)
        mask_blocks += ref.shape[0]
    turned = jnp.transpose(small[:, 0:HD])
    rows_in[...] = spread_blocks(turned[0 : rows_in.shape[0], :], mask_blocks)
    rows_out[...] = spread_blocks(mask_out_ref[...].astype(F32), mask_out_ref.shape[1])

    def mask_tiles(weight, rows):
        def step(i, carry):
            at = pl.ds(pl.multiple_of(i * TILE, TILE), TILE)
            kept = jnp.broadcast_to(rows[pl.ds(i, 1), :], (16, rows.shape[1])).astype(BF16)
            tile = weight[at, :].reshape(TILE // 16, 16, rows.shape[1])
            weight[at, :] = (tile * kept[None]).reshape(TILE, rows.shape[1])
            return carry

        lax.fori_loop(0, rows.shape[0], step, 0)

    for copy in weight_copies[:3]:
        copy.wait()
    mask_tiles(w_in, rows_in)
    weight_copies[3].wait()
    mask_tiles(w_o, rows_out)

    row = lax.broadcasted_iota(jnp.int32, (span, span), 0)
    col = lax.broadcasted_iota(jnp.int32, (span, span), 1)
    log_rows = jnp.dot(
        jnp.log(decay_ref[...]),
        jnp.where(row <= col, 1.0, 0.0),
        precision=lax.Precision.HIGHEST,
        preferred_element_type=F32,
    )
    small[0:heads, :] = log_rows
    log_rows_ref[...] = log_rows
    columns_ref[...] = jnp.transpose(small[...])

    def forward(step):
        token_pushes[step].wait_recv()
        held = tok.at[lax.rem(y + chips_y - step, chips_y) * CORES + core]
        copy = push(held, held, sib_send_sem.at[step], sib_recv_sem.at[step], sibling)
        copy.start()
        sibling_pushes[step] = copy

    def project_in(steps):
        slots = [
            lax.rem(y + chips_y - step, chips_y) * CORES + which for step in steps for which in range(CORES)
        ]
        rows = jnp.concatenate([tok[slot] for slot in slots], axis=0)
        raw = jnp.dot(rows, w_in[...], preferred_element_type=F32)
        beta = jax.nn.sigmoid(mm_nt(rows, w_beta_ref[...]))
        parts = []
        for i in range(key_heads):
            query = unit_rows(raw[:, i * HD : (i + 1) * HD])
            parts.append((query * (1.0 / math.sqrt(HD))).astype(BF16))
        for i in range(key_heads):
            parts.append(unit_rows(raw[:, key_cols + i * HD : key_cols + (i + 1) * HD]).astype(BF16))
        parts.append(jax.nn.silu(raw[:, 2 * key_cols : in_cols]).astype(BF16))
        made = jnp.concatenate(parts, axis=1)
        for n, slot in enumerate(slots):
            qkv[slot] = made[n * piece : (n + 1) * piece]
            beta_out[slot] = beta[n * piece : (n + 1) * piece]

    near = [step for step in far_first if min(step, chips_y - step) == 1]
    far = [step for step in far_first if min(step, chips_y - step) > 1]
    for step in near + far:
        forward(step)
    for step in [0] + near:
        sibling_pushes[step].wait_recv()
    project_in([0] + near)
    if far:
        for step in far:
            sibling_pushes[step].wait_recv()
        project_in(far)

    for step in far_first:
        token_pushes[step].wait_send()
    for copy in sibling_pushes.values():
        copy.wait_send()


def state_kernel(
    seq_count,
    head_count,
    qkv,
    beta_out,
    w_o,
    log_rows_ref,
    columns_ref,
    gain_hbm,
    out_ref,
    gain_ref,
    w_o_other,
    local_out,
    local_q,
    ab_send,
    ab_recv,
    x_send,
    x_recv,
    s_send,
    s_recv,
    hidden,
    hidden_other,
    own_part,
    sum_send,
    sum_recv,
    small_sem,
    ab_send_sem,
    ab_recv_sem,
    x_send_sem,
    x_recv_sem,
    s_send_sem,
    s_recv_sem,
    other_send_sem,
    other_recv_sem,
    sum_send_sem,
    sum_recv_sem,
):
    s = lax.axis_index("seq")
    hd = lax.axis_index("head")
    chips_x = seq_count // RING
    chips_y = head_count // CORES
    x, z = s // RING, lax.rem(s, RING)
    y, core = hd // CORES, lax.rem(hd, CORES)
    _, piece, in_cols = qkv.shape
    value_cols, width = w_o.shape
    span = piece * head_count
    key_cols = (in_cols - value_cols) // 2
    heads = value_cols // HD
    key_heads = key_cols // HD

    def at_y(step):
        return (s, lax.rem(y + step, chips_y) * CORES + core)

    sibling = (s, y * CORES + (1 - core))

    def at_z(place):
        return (x * RING + place, hd)

    def at_x(step):
        return (lax.rem(x + step, chips_x) * RING + z, hd)

    far_first = far_first_steps(chips_y)
    far_first_x = far_first_steps(chips_x)
    wait_partners = greet(
        [at_z(lax.rem(z + step, RING)) for step in far_first_steps(RING)]
        + [at_x(step) for step in far_first_x]
        + [at_y(step) for step in far_first]
        + [sibling]
    )
    gain_copy = pltpu.make_async_copy(gain_hbm, gain_ref, small_sem.at[0])
    gain_copy.start()
    row = lax.broadcasted_iota(jnp.int32, (span, span), 0)
    col = lax.broadcasted_iota(jnp.int32, (span, span), 1)
    log_rows = log_rows_ref[...]
    columns = columns_ref[...]

    made = qkv[...].reshape(span, in_cols)
    beta_cols = beta_out[...].reshape(span, heads)
    queries, keys, key_turned, grams, pair_scores = [], [], [], [], []
    for i in range(key_heads):
        query = made[:, i * HD : (i + 1) * HD]
        key = made[:, key_cols + i * HD : key_cols + (i + 1) * HD]
        queries.append(query.astype(F32))
        keys.append(key.astype(F32))
        key_turned.append(jnp.transpose(key.astype(F32)))
        grams.append(mm_nt(key, key))
        pair_scores.append(mm_nt(query, key))
    values = made[:, 2 * key_cols : in_cols].astype(F32)

    eye = jnp.where(
        lax.broadcasted_iota(jnp.int32, (HD, HD), 0) == lax.broadcasted_iota(jnp.int32, (HD, HD), 1),
        1.0,
        0.0,
    )
    is_root = lax.rem(z, CORES) == core

    def key_head(h):
        return h * key_heads // heads

    ab_pushes = []
    far_first_heads = sorted(range(heads), key=lambda turn: -min(turn, heads - turn))
    members = range(heads)
    lasts = [log_rows[h : h + 1, span - 1 : span] for h in members]
    rises = [jnp.exp(columns[:, h : h + 1]) for h in members]
    betas = [beta_cols[:, h : h + 1] for h in members]
    decays = [
        jnp.where(
            row >= col,
            jnp.exp(jnp.where(row >= col, columns[:, h : h + 1] - log_rows[h : h + 1, :], 0.0)),
            0.0,
        )
        for h in members
    ]
    inverses = unit_lower_inverses(
        [
            jnp.where(row > col, beta * decay * grams[key_head(h)], 0.0)
            for h, beta, decay in zip(members, betas, decays)
        ],
        row,
        col,
    )
    mixes = [
        mm(
            inverse,
            jnp.concatenate(
                [
                    ((beta * rise) * keys[key_head(h)]).astype(BF16),
                    (beta * values[:, h * HD : (h + 1) * HD]).astype(BF16),
                ],
                axis=1,
            ),
        ).astype(BF16)
        for h, inverse, beta, rise in zip(members, inverses, betas, rises)
    ]
    ends = [
        mm(key_turned[key_head(h)] * jnp.exp(last - log_rows[h : h + 1, :]), mixed)
        for h, last, mixed in zip(members, lasts, mixes)
    ]
    for h, last, end in zip(members, lasts, ends):
        transition = jnp.exp(last) * eye - end[:, 0:HD]
        ab_send[h] = jnp.concatenate([transition, end[:, HD : 2 * HD]], axis=1).astype(BF16)

    wait_partners()
    for turn in far_first_heads:
        h = lax.rem(z // CORES + turn, heads)
        target = h * CORES + core
        copy = push(ab_send.at[h], ab_recv.at[z], ab_send_sem.at[turn], ab_recv_sem.at[z], at_z(target))
        ab_pushes.append((turn, copy))
        if turn:
            copy.start()
        else:
            pl.when(jnp.logical_not(is_root))(copy.start)

    @pl.when(is_root)
    def _():
        ab_recv[z] = ab_send[z // CORES]

    w_o_push = push(w_o, w_o_other, other_send_sem.at[0], other_recv_sem.at[0], sibling)
    w_o_push.start()

    reads = [
        mm(pair_scores[key_head(h)] * decay, mixed) for h, decay, mixed in zip(members, decays, mixes)
    ]
    for h, rise, read in zip(members, rises, reads):
        local_out[h] = read[:, HD : 2 * HD]
        local_q[h] = (rise * queries[key_head(h)] - read[:, 0:HD]).astype(BF16)

    def ring_step(step):
        return lax.rem(z + step, RING)

    def s_push(step):
        mine, place = z // CORES, ring_step(step)
        return push(
            s_send.at[place], s_recv.at[mine], s_send_sem.at[step], s_recv_sem.at[mine], at_z(place)
        )

    def after(later, earlier):
        both = mm(later[:, 0:HD], earlier)
        return jnp.concatenate(
            [both[:, 0:HD], both[:, HD : 2 * HD] + later[:, HD : 2 * HD].astype(F32)], axis=1
        )

    def advance(pair, state):
        return mm(pair[:, 0:HD], state) + pair[:, HD : 2 * HD].astype(F32)

    far_first_z = far_first_steps(RING)

    @pl.when(is_root)
    def _():
        for step in reversed(far_first_z):
            place = ring_step(step)
            push(
                ab_send.at[0], ab_recv.at[place], ab_send_sem.at[0], ab_recv_sem.at[place], at_z(place)
            ).wait_recv()
        pairs = [ab_recv[place] for place in range(RING)]
        level = {(place, place + 1): pairs[place] for place in range(RING)}
        size = 1
        while size < RING:
            for low in range(0, RING, 2 * size):
                level[low, low + 2 * size] = after(
                    level[low + size, low + 2 * size], level[low, low + size]
                ).astype(BF16)
            size *= 2
        x_send[...] = level[0, RING]
        x_pushes = {
            step: push(x_send, x_recv.at[x], x_send_sem.at[step], x_recv_sem.at[step], at_x(step))
            for step in far_first_x
        }
        for step, copy in x_pushes.items():
            pl.when(x + step < chips_x)(copy.start)
        prefixes = []
        for end in range(1, RING):
            low, total = 0, None
            for size in (4, 2, 1):
                if end & size:
                    part = level[low, low + size]
                    total = part if total is None else after(part, total).astype(BF16)
                    low += size
            prefixes.append(total)
        for step in far_first_x:
            earlier = push(
                x_send, x_recv.at[x - step], x_send_sem.at[step], x_recv_sem.at[step], at_x(step)
            )
            pl.when(x >= step)(earlier.wait_recv)
        state = jnp.where(x > 0, x_recv[0, :, HD : 2 * HD].astype(F32), 0.0)
        for place in range(1, chips_x - 1):
            state = jnp.where(place < x, advance(x_recv[place], state), state)
        s_send[0] = state.astype(BF16)
        for place in range(1, RING):
            s_send[place] = advance(prefixes[place - 1], state).astype(BF16)
        for step in far_first_z:
            s_push(step).start()
        s_recv[z // CORES] = s_send[z]
        for step, copy in x_pushes.items():
            pl.when(x + step < chips_x)(copy.wait_send)
        for step in far_first_z:
            s_push(step).wait_send()

    gain_copy.wait()
    for h in range(heads):
        source = h * CORES + core

        @pl.when(z != source)
        def _():
            push(
                s_send.at[0], s_recv.at[h], s_send_sem.at[0], s_recv_sem.at[h], at_z(source)
            ).wait_recv()

        state_out = local_out[h] + jnp.dot(local_q[h], s_recv[h], preferred_element_type=F32)
        inv_rms = lax.rsqrt(jnp.mean(state_out * state_out, -1, keepdims=True) + 1e-06)
        hidden[:, :, :, h * HD : (h + 1) * HD] = (
            (state_out * inv_rms * gain_ref[...]).astype(BF16).reshape(chips_y, CORES, piece, HD)
        )

    hidden_push = push(
        hidden.at[:, 1 - core], hidden_other, other_send_sem.at[1], other_recv_sem.at[1], sibling
    )
    hidden_push.start()
    order = far_first + [0]
    places = [lax.rem(y + step, chips_y) for step in order]
    own_rows = jnp.concatenate([hidden[place, core] for place in places], axis=0)
    own_part[...] = jnp.dot(own_rows, w_o[...], preferred_element_type=F32).reshape(chips_y, piece, width)
    w_o_push.wait_recv()
    hidden_push.wait_recv()
    sum_pushes = []
    half = max(chips_y // 2, 1)
    for first in range(0, chips_y, half):
        members = range(first, first + half)
        rows = jnp.concatenate([hidden_other[places[n]] for n in members], axis=0)
        both = jnp.dot(rows, w_o_other[...], preferred_element_type=F32).reshape(half, piece, width)
        both = both + own_part[first : first + half]
        for n in members:
            if order[n] == 0:
                total = both[n - first]
            else:
                sum_send[n] = both[n - first].astype(BF16)
                copy = push(
                    sum_send.at[n], sum_recv.at[n], sum_send_sem.at[n], sum_recv_sem.at[n], at_y(order[n])
                )
                copy.start()
                sum_pushes.append(copy)
    for n, copy in enumerate(sum_pushes):
        copy.wait_recv()
        total = total + sum_recv[n].astype(F32)
    out_ref[...] = total.astype(BF16)

    for copy in sum_pushes + [w_o_push, hidden_push]:
        copy.wait_send()
    for turn, copy in ab_pushes:
        if turn:
            copy.wait_send()
        else:
            pl.when(jnp.logical_not(is_root))(copy.wait_send)


def on_device(
    seq_count,
    head_count,
    tokens,
    w_query,
    w_key,
    w_value,
    w_beta,
    w_out,
    mask_query,
    mask_key,
    mask_value,
    mask_out,
    decay_rate,
    norm_gain,
):
    piece, width = tokens.shape
    span = piece * head_count
    value_cols = w_value.shape[1]
    in_cols = 2 * w_query.shape[1] + value_cols
    heads = value_cols // HD
    chips_x = seq_count // RING
    chips_y = head_count // CORES
    vmem = pl.BlockSpec(memory_space=pltpu.VMEM)
    hbm = pl.BlockSpec(memory_space=pltpu.HBM)
    dma = pltpu.SemaphoreType.DMA

    def in_hbm(array):
        return pltpu.with_memory_space_constraint(array, pltpu.HBM)

    made = pl.pallas_call(
        functools.partial(gather_kernel, head_count),
        out_shape=[
            pltpu.VMEM((head_count, piece, in_cols), BF16),
            pltpu.VMEM((head_count, piece, heads), F32),
            pltpu.VMEM((value_cols, width), BF16),
            pltpu.VMEM((heads, span), F32),
            pltpu.VMEM((span, HD), F32),
        ],
        in_specs=[hbm] * 11,
        out_specs=[vmem] * 5,
        scratch_shapes=[
            pltpu.VMEM((heads, width), BF16),
            pltpu.VMEM(mask_query.shape[::-1], jnp.int32),
            pltpu.VMEM(mask_key.shape[::-1], jnp.int32),
            pltpu.VMEM(mask_value.shape[::-1], jnp.int32),
            pltpu.VMEM(mask_out.shape, jnp.int32),
            pltpu.VMEM((heads, span), F32),
            pltpu.VMEM((width, in_cols), BF16),
            pltpu.VMEM((head_count, piece, width), BF16),
            pltpu.VMEM((HD, span), F32),
            pltpu.VMEM((width // TILE, in_cols), F32),
            pltpu.VMEM((value_cols // TILE, width), F32),
            dma((4,)),
            dma((7,)),
            dma((chips_y,)),
            dma((chips_y,)),
            dma((chips_y,)),
            dma((chips_y,)),
        ],
        compiler_params=pltpu.CompilerParams(
            collective_id=0, has_side_effects=True, vmem_limit_bytes=40 * 1024 * 1024
        ),
        name="gather",
    )(
        *(
            in_hbm(array)
            for array in (
                tokens,
                w_query,
                w_key,
                w_value,
                w_beta.T,
                w_out,
                mask_query.T,
                mask_key.T,
                mask_value.T,
                mask_out,
                decay_rate.T,
            )
        )
    )
    return pl.pallas_call(
        functools.partial(state_kernel, seq_count, head_count),
        out_shape=pltpu.VMEM((piece, width), BF16),
        in_specs=[vmem] * 5 + [hbm],
        out_specs=vmem,
        scratch_shapes=[
            pltpu.VMEM((1, HD), F32),
            pltpu.VMEM((value_cols, width), BF16),
            pltpu.VMEM((heads, span, HD), F32),
            pltpu.VMEM((heads, span, HD), BF16),
            pltpu.VMEM((heads, HD, 2 * HD), BF16),
            pltpu.VMEM((RING, HD, 2 * HD), BF16),
            pltpu.VMEM((HD, 2 * HD), BF16),
            pltpu.VMEM((chips_x, HD, 2 * HD), BF16),
            pltpu.VMEM((RING, HD, HD), BF16),
            pltpu.VMEM((heads, HD, HD), BF16),
            pltpu.VMEM((chips_y, CORES, piece, value_cols), BF16),
            pltpu.VMEM((chips_y, piece, value_cols), BF16),
            pltpu.VMEM((chips_y, piece, width), F32),
            pltpu.VMEM((chips_y - 1, piece, width), BF16),
            pltpu.VMEM((chips_y - 1, piece, width), BF16),
            dma((1,)),
            dma((heads,)),
            dma((RING,)),
            dma((chips_x,)),
            dma((chips_x,)),
            dma((RING,)),
            dma((heads,)),
            dma((2,)),
            dma((2,)),
            dma((chips_y - 1,)),
            dma((chips_y - 1,)),
        ],
        compiler_params=pltpu.CompilerParams(
            collective_id=1, has_side_effects=True, vmem_limit_bytes=40 * 1024 * 1024
        ),
        name="state",
    )(*made, in_hbm(norm_gain.reshape(1, HD)))


def solution(mesh):
    return jax.shard_map(
        functools.partial(on_device, mesh.shape["seq"], mesh.shape["head"]),
        mesh=mesh,
        in_specs=(
            P(("seq", "head"), None),
            P(None, "head"),
            P(None, "head"),
            P(None, "head"),
            P(None, "head"),
            P("head", None),
            P(None, "head"),
            P(None, "head"),
            P(None, "head"),
            P("head", None),
            P("seq", "head"),
            P(),
        ),
        out_specs=P(("seq", "head"), None),
        check_vma=False,
    )
```

```python
import functools
import math

import jax
import jax.numpy as jnp
from jax import lax
from jax.experimental import pallas as pl
from jax.experimental.pallas import tpu as pltpu
from jax.sharding import PartitionSpec as P

HD = 128
TILE = 64
RING = 8
CORES = 2
MESH = pl.DeviceIdType.MESH
F32 = jnp.float32
BF16 = jnp.bfloat16


def mm(left, right):
    return jnp.dot(left.astype(BF16), right.astype(BF16), preferred_element_type=F32)


def mm_nt(left, right):
    return lax.dot_general(
        left, right, (((1,), (1,)), ((), ())), preferred_element_type=F32
    )


def unit_rows(matrix):
    return matrix * lax.rsqrt(jnp.sum(matrix * matrix, -1, keepdims=True) + 1e-06)


def spread_blocks(columns, count):
    rows = columns.shape[0]
    first = lax.broadcasted_iota(jnp.int32, (rows, 2 * TILE), 1) < TILE
    return jnp.concatenate(
        [
            jnp.where(first, columns[:, 2 * i : 2 * i + 1], columns[:, 2 * i + 1 : 2 * i + 2])
            for i in range(count // 2)
        ],
        axis=1,
    )


def corner_masks(row, col):
    masks = [row == col]
    shift = 0
    while (1 << shift) < row.shape[0]:
        masks.append(
            ((row >> (shift + 1)) == (col >> (shift + 1))) & ((row >> shift) != (col >> shift)) & (row > col)
        )
        shift += 1
    return masks


def unit_lower_inverses(negated, masks):
    inverses = [masks[0] + lower * masks[1] for lower in negated]
    for n in range(2, masks.shape[0]):
        corner = masks[n]
        halves = [mm(inverse, lower * corner).astype(BF16) for inverse, lower in zip(inverses, negated)]
        inverses = [inverse + mm(half, inverse).astype(BF16) for inverse, half in zip(inverses, halves)]
    return inverses


def push(source, target, send_sem, recv_sem, device):
    return pltpu.make_async_remote_copy(
        src_ref=source,
        dst_ref=target,
        send_sem=send_sem,
        recv_sem=recv_sem,
        device_id=device,
        device_id_type=MESH,
    )


def greet(partners):
    barrier = pltpu.get_barrier_semaphore()
    for partner in partners:
        pl.semaphore_signal(barrier, inc=1, device_id=partner, device_id_type=MESH)
    return lambda: pl.semaphore_wait(barrier, len(partners))


def far_first_steps(count):
    return sorted(range(1, count), key=lambda step: -min(step, count - step))


def near_and_far(chips_y):
    steps = far_first_steps(chips_y)
    far = [step for step in steps if min(step, chips_y - step) > 1]
    return [step for step in steps if step not in far], far


def chip_slots(y, chips_y, steps):
    return [lax.rem(y + chips_y - step, chips_y) * CORES + core for step in steps for core in range(CORES)]


def project(rows, w_in, w_beta, key_cols):
    raw = jnp.dot(rows, w_in[...], preferred_element_type=F32)
    beta = jax.nn.sigmoid(mm_nt(rows, w_beta[...]))
    parts = []
    for at in range(0, key_cols, HD):
        parts.append((unit_rows(raw[:, at : at + HD]) * (1.0 / math.sqrt(HD))).astype(BF16))
    for at in range(key_cols, 2 * key_cols, HD):
        parts.append(unit_rows(raw[:, at : at + HD]).astype(BF16))
    parts.append(jax.nn.silu(raw[:, 2 * key_cols :]).astype(BF16))
    return jnp.concatenate(parts, axis=1), beta


def gather_kernel(
    head_count,
    tokens_ref,
    w_query_ref,
    w_key_ref,
    w_value_ref,
    w_beta_hbm,
    w_out_ref,
    mask_query_hbm,
    mask_key_hbm,
    mask_value_hbm,
    mask_out_hbm,
    decay_hbm,
    qkv,
    beta_out,
    w_o,
    log_rows_ref,
    columns_ref,
    decays_ref,
    masks_ref,
    far_rows,
    w_in,
    w_beta_ref,
    mask_query_ref,
    mask_key_ref,
    mask_value_ref,
    mask_out_ref,
    decay_ref,
    tok,
    small,
    rows_in,
    rows_out,
    w_sem,
    small_sem,
    tok_send_sem,
    tok_recv_sem,
    sib_send_sem,
    sib_recv_sem,
):
    s = lax.axis_index("seq")
    hd = lax.axis_index("head")
    chips_y = head_count // CORES
    y, core = hd // CORES, lax.rem(hd, CORES)
    piece, width = tokens_ref.shape
    span = piece * head_count
    key_cols = w_query_ref.shape[1]
    value_cols = w_value_ref.shape[1]
    heads = value_cols // HD
    key_heads = key_cols // HD
    in_cols = 2 * key_cols + value_cols

    def at_y(step):
        return (s, lax.rem(y + step, chips_y) * CORES + core)

    sibling = (s, y * CORES + (1 - core))
    far_first = far_first_steps(chips_y)
    wait_partners = greet([at_y(step) for step in range(1, chips_y)] + [sibling])

    small_copies = [
        pltpu.make_async_copy(source, target, small_sem.at[n])
        for n, (source, target) in enumerate(
            (
                (mask_query_hbm, mask_query_ref),
                (mask_key_hbm, mask_key_ref),
                (mask_value_hbm, mask_value_ref),
                (mask_out_hbm, mask_out_ref),
                (w_beta_hbm, w_beta_ref),
                (decay_hbm, decay_ref),
                (tokens_ref, tok.at[hd]),
            )
        )
    ]
    for copy in small_copies:
        copy.start()
    weight_copies = [
        pltpu.make_async_copy(w_query_ref, w_in.at[:, pl.ds(0, key_cols)], w_sem.at[0]),
        pltpu.make_async_copy(w_key_ref, w_in.at[:, pl.ds(key_cols, key_cols)], w_sem.at[1]),
        pltpu.make_async_copy(w_value_ref, w_in.at[:, pl.ds(2 * key_cols, value_cols)], w_sem.at[2]),
        pltpu.make_async_copy(w_out_ref, w_o, w_sem.at[3]),
    ]
    for copy in weight_copies:
        copy.start()
    wait_partners()

    token_pushes = {
        step: push(
            tokens_ref, tok.at[hd], tok_send_sem.at[step], tok_recv_sem.at[step], at_y(step)
        )
        for step in far_first
    }
    for step in reversed(far_first):
        token_pushes[step].start()
    sibling_pushes = {
        0: push(tokens_ref, tok.at[hd], sib_send_sem.at[0], sib_recv_sem.at[0], sibling)
    }
    sibling_pushes[0].start()

    for copy in small_copies:
        copy.wait()
    small[...] = jnp.zeros_like(small)
    mask_blocks = 0
    for ref in (mask_query_ref, mask_key_ref, mask_value_ref):
        small[mask_blocks : mask_blocks + ref.shape[0], 0 : ref.shape[1]] = ref[...].astype(F32)
        mask_blocks += ref.shape[0]
    turned = jnp.transpose(small[:, 0:HD])
    rows_in[...] = spread_blocks(turned[0 : rows_in.shape[0], :], mask_blocks)
    rows_out[...] = spread_blocks(mask_out_ref[...].astype(F32), mask_out_ref.shape[1])

    def mask_tiles(weight, rows):
        def step(i, carry):
            at = pl.ds(pl.multiple_of(i * TILE, TILE), TILE)
            kept = jnp.broadcast_to(rows[pl.ds(i, 1), :], (16, rows.shape[1])).astype(BF16)
            tile = weight[at, :].reshape(TILE // 16, 16, rows.shape[1])
            weight[at, :] = (tile * kept[None]).reshape(TILE, rows.shape[1])
            return carry

        lax.fori_loop(0, rows.shape[0], step, 0)

    for copy in weight_copies[:3]:
        copy.wait()
    mask_tiles(w_in, rows_in)
    weight_copies[3].wait()
    mask_tiles(w_o, rows_out)

    row = lax.broadcasted_iota(jnp.int32, (span, span), 0)
    col = lax.broadcasted_iota(jnp.int32, (span, span), 1)
    log_rows = jnp.dot(
        jnp.log(decay_ref[...]),
        jnp.where(row <= col, 1.0, 0.0),
        precision=lax.Precision.HIGHEST,
        preferred_element_type=F32,
    )
    small[0:heads, :] = log_rows
    columns = jnp.transpose(small[...])
    log_rows_ref[...] = log_rows
    columns_ref[...] = columns

    def forward(step):
        token_pushes[step].wait_recv()
        held = tok.at[lax.rem(y + chips_y - step, chips_y) * CORES + core]
        copy = push(held, held, sib_send_sem.at[step], sib_recv_sem.at[step], sibling)
        copy.start()
        sibling_pushes[step] = copy

    def slots_of(steps):
        return chip_slots(y, chips_y, steps)

    near, far = near_and_far(chips_y)
    for step in near:
        forward(step)
    for n, mask in enumerate(corner_masks(row, col)):
        masks_ref[n] = jnp.where(mask, 1.0, 0.0).astype(BF16)
    for h in range(heads):
        spread = jnp.where(row >= col, columns[:, h : h + 1] - log_rows[h : h + 1, :], 0.0)
        decays_ref[h] = jnp.where(row >= col, jnp.exp(spread), 0.0)
    for step in far:
        forward(step)
    for step in [0] + near:
        sibling_pushes[step].wait_recv()
    slots = slots_of([0] + near)
    rows = jnp.concatenate([tok[slot] for slot in slots], axis=0)
    made, beta = project(rows, w_in, w_beta_ref, key_cols)
    for n, slot in enumerate(slots):
        qkv[slot] = made[n * piece : (n + 1) * piece]
        beta_out[slot] = beta[n * piece : (n + 1) * piece]
    for step in far:
        sibling_pushes[step].wait_recv()
    for n, slot in enumerate(slots_of(far)):
        far_rows[n] = tok[slot]

    for step in far_first:
        token_pushes[step].wait_send()
    for copy in sibling_pushes.values():
        copy.wait_send()


def state_kernel(
    seq_count,
    head_count,
    qkv,
    beta_out,
    w_o,
    log_rows_ref,
    columns_ref,
    decays_ref,
    masks_ref,
    far_rows,
    w_in,
    w_beta_ref,
    gain_hbm,
    out_ref,
    gain_ref,
    qkv_all,
    beta_all,
    w_o_other,
    local_out,
    local_q,
    ab_send,
    ab_recv,
    x_send,
    x_recv,
    s_send,
    s_recv,
    hidden,
    hidden_other,
    own_part,
    sum_send,
    sum_recv,
    small_sem,
    ab_send_sem,
    ab_recv_sem,
    x_send_sem,
    x_recv_sem,
    s_send_sem,
    s_recv_sem,
    other_send_sem,
    other_recv_sem,
    sum_send_sem,
    sum_recv_sem,
):
    s = lax.axis_index("seq")
    hd = lax.axis_index("head")
    chips_x = seq_count // RING
    chips_y = head_count // CORES
    x, z = s // RING, lax.rem(s, RING)
    y, core = hd // CORES, lax.rem(hd, CORES)
    _, piece, in_cols = qkv.shape
    value_cols, width = w_o.shape
    span = piece * head_count
    key_cols = (in_cols - value_cols) // 2
    heads = value_cols // HD
    key_heads = key_cols // HD

    def at_y(step):
        return (s, lax.rem(y + step, chips_y) * CORES + core)

    sibling = (s, y * CORES + (1 - core))

    def at_z(place):
        return (x * RING + place, hd)

    def at_x(step):
        return (lax.rem(x + step, chips_x) * RING + z, hd)

    far_first = far_first_steps(chips_y)
    far_first_x = far_first_steps(chips_x)
    wait_partners = greet(
        [at_z(lax.rem(z + step, RING)) for step in far_first_steps(RING)]
        + [at_x(step) for step in far_first_x]
        + [at_y(step) for step in far_first]
        + [sibling]
    )
    gain_copy = pltpu.make_async_copy(gain_hbm, gain_ref, small_sem.at[0])
    gain_copy.start()
    row = lax.broadcasted_iota(jnp.int32, (span, span), 0)
    col = lax.broadcasted_iota(jnp.int32, (span, span), 1)
    log_rows = log_rows_ref[...]
    columns = columns_ref[...]

    qkv_all[...] = qkv[...]
    beta_all[...] = beta_out[...]
    _, far = near_and_far(chips_y)
    if far:
        slots = chip_slots(y, chips_y, far)
        rows = far_rows[...].reshape(len(slots) * piece, width)
        made, beta = project(rows, w_in, w_beta_ref, key_cols)
        for n, slot in enumerate(slots):
            qkv_all[slot] = made[n * piece : (n + 1) * piece]
            beta_all[slot] = beta[n * piece : (n + 1) * piece]
    made = qkv_all[...].reshape(span, in_cols)
    beta_cols = beta_all[...].reshape(span, heads)
    queries, keys, key_turned, grams, pair_scores = [], [], [], [], []
    for i in range(key_heads):
        query = made[:, i * HD : (i + 1) * HD]
        key = made[:, key_cols + i * HD : key_cols + (i + 1) * HD]
        queries.append(query.astype(F32))
        keys.append(key.astype(F32))
        key_turned.append(jnp.transpose(key.astype(F32)))
        grams.append(mm_nt(key, key))
        pair_scores.append(mm_nt(query, key))
    values = made[:, 2 * key_cols : in_cols].astype(F32)

    eye = jnp.where(
        lax.broadcasted_iota(jnp.int32, (HD, HD), 0) == lax.broadcasted_iota(jnp.int32, (HD, HD), 1),
        1.0,
        0.0,
    )
    is_root = lax.rem(z, CORES) == core

    def key_head(h):
        return h * key_heads // heads

    ab_pushes = []
    far_first_heads = sorted(range(heads), key=lambda turn: -min(turn, heads - turn))
    members = range(heads)
    lasts = [log_rows[h : h + 1, span - 1 : span] for h in members]
    rises = [jnp.exp(columns[:, h : h + 1]) for h in members]
    betas = [beta_cols[:, h : h + 1] for h in members]
    decays = [decays_ref[h] for h in members]
    inverses = unit_lower_inverses(
        [
            jnp.where(row > col, -beta * decay * grams[key_head(h)], 0.0).astype(BF16)
            for h, beta, decay in zip(members, betas, decays)
        ],
        masks_ref,
    )
    mixes = [
        mm(
            inverse,
            jnp.concatenate(
                [
                    ((beta * rise) * keys[key_head(h)]).astype(BF16),
                    (beta * values[:, h * HD : (h + 1) * HD]).astype(BF16),
                ],
                axis=1,
            ),
        ).astype(BF16)
        for h, inverse, beta, rise in zip(members, inverses, betas, rises)
    ]
    ends = [
        mm(key_turned[key_head(h)] * jnp.exp(last - log_rows[h : h + 1, :]), mixed)
        for h, last, mixed in zip(members, lasts, mixes)
    ]
    for h, last, end in zip(members, lasts, ends):
        transition = jnp.exp(last) * eye - end[:, 0:HD]
        ab_send[h] = jnp.concatenate([transition, end[:, HD : 2 * HD]], axis=1).astype(BF16)

    wait_partners()
    for turn in far_first_heads:
        h = lax.rem(z // CORES + turn, heads)
        target = h * CORES + core
        copy = push(ab_send.at[h], ab_recv.at[z], ab_send_sem.at[turn], ab_recv_sem.at[z], at_z(target))
        ab_pushes.append((turn, copy))
        if turn:
            copy.start()
        else:
            pl.when(jnp.logical_not(is_root))(copy.start)

    @pl.when(is_root)
    def _():
        ab_recv[z] = ab_send[z // CORES]

    w_o_push = push(w_o, w_o_other, other_send_sem.at[0], other_recv_sem.at[0], sibling)
    w_o_push.start()

    reads = [
        mm(pair_scores[key_head(h)] * decay, mixed) for h, decay, mixed in zip(members, decays, mixes)
    ]
    for h, rise, read in zip(members, rises, reads):
        local_out[h] = read[:, HD : 2 * HD]
        local_q[h] = (rise * queries[key_head(h)] - read[:, 0:HD]).astype(BF16)

    def ring_step(step):
        return lax.rem(z + step, RING)

    def s_push(step):
        mine, place = z // CORES, ring_step(step)
        return push(
            s_send.at[place], s_recv.at[mine], s_send_sem.at[step], s_recv_sem.at[mine], at_z(place)
        )

    def after(later, earlier):
        both = mm(later[:, 0:HD], earlier)
        return jnp.concatenate(
            [both[:, 0:HD], both[:, HD : 2 * HD] + later[:, HD : 2 * HD].astype(F32)], axis=1
        )

    def advance(pair, state):
        return mm(pair[:, 0:HD], state) + pair[:, HD : 2 * HD].astype(F32)

    far_first_z = far_first_steps(RING)

    @pl.when(is_root)
    def _():
        for step in reversed(far_first_z):
            place = ring_step(step)
            push(
                ab_send.at[0], ab_recv.at[place], ab_send_sem.at[0], ab_recv_sem.at[place], at_z(place)
            ).wait_recv()
        pairs = [ab_recv[place] for place in range(RING)]
        level = {(place, place + 1): pairs[place] for place in range(RING)}
        size = 1
        while size < RING:
            for low in range(0, RING, 2 * size):
                level[low, low + 2 * size] = after(
                    level[low + size, low + 2 * size], level[low, low + size]
                ).astype(BF16)
            size *= 2
        x_send[...] = level[0, RING]
        x_pushes = {
            step: push(x_send, x_recv.at[x], x_send_sem.at[step], x_recv_sem.at[step], at_x(step))
            for step in far_first_x
        }
        for step, copy in x_pushes.items():
            pl.when(x + step < chips_x)(copy.start)
        prefixes = []
        for end in range(1, RING):
            low, total = 0, None
            for size in (4, 2, 1):
                if end & size:
                    part = level[low, low + size]
                    total = part if total is None else after(part, total).astype(BF16)
                    low += size
            prefixes.append(total)
        for step in far_first_x:
            earlier = push(
                x_send, x_recv.at[x - step], x_send_sem.at[step], x_recv_sem.at[step], at_x(step)
            )
            pl.when(x >= step)(earlier.wait_recv)
        state = jnp.where(x > 0, x_recv[0, :, HD : 2 * HD].astype(F32), 0.0)
        for place in range(1, chips_x - 1):
            state = jnp.where(place < x, advance(x_recv[place], state), state)
        s_send[0] = state.astype(BF16)
        for place in range(1, RING):
            s_send[place] = advance(prefixes[place - 1], state).astype(BF16)
        for step in far_first_z:
            s_push(step).start()
        s_recv[z // CORES] = s_send[z]
        for step, copy in x_pushes.items():
            pl.when(x + step < chips_x)(copy.wait_send)
        for step in far_first_z:
            s_push(step).wait_send()

    gain_copy.wait()
    for h in range(heads):
        source = h * CORES + core

        @pl.when(z != source)
        def _():
            push(
                s_send.at[0], s_recv.at[h], s_send_sem.at[0], s_recv_sem.at[h], at_z(source)
            ).wait_recv()

        state_out = local_out[h] + jnp.dot(local_q[h], s_recv[h], preferred_element_type=F32)
        inv_rms = lax.rsqrt(jnp.mean(state_out * state_out, -1, keepdims=True) + 1e-06)
        hidden[:, :, :, h * HD : (h + 1) * HD] = (
            (state_out * inv_rms * gain_ref[...]).astype(BF16).reshape(chips_y, CORES, piece, HD)
        )

    hidden_push = push(
        hidden.at[:, 1 - core], hidden_other, other_send_sem.at[1], other_recv_sem.at[1], sibling
    )
    hidden_push.start()
    order = far_first + [0]
    places = [lax.rem(y + step, chips_y) for step in order]
    own_rows = jnp.concatenate([hidden[place, core] for place in places], axis=0)
    own_part[...] = jnp.dot(own_rows, w_o[...], preferred_element_type=F32).reshape(chips_y, piece, width)
    w_o_push.wait_recv()
    hidden_push.wait_recv()
    sum_pushes = []
    half = max(chips_y // 2, 1)
    for first in range(0, chips_y, half):
        members = range(first, first + half)
        rows = jnp.concatenate([hidden_other[places[n]] for n in members], axis=0)
        both = jnp.dot(rows, w_o_other[...], preferred_element_type=F32).reshape(half, piece, width)
        both = both + own_part[first : first + half]
        for n in members:
            if order[n] == 0:
                total = both[n - first]
            else:
                sum_send[n] = both[n - first].astype(BF16)
                copy = push(
                    sum_send.at[n], sum_recv.at[n], sum_send_sem.at[n], sum_recv_sem.at[n], at_y(order[n])
                )
                copy.start()
                sum_pushes.append(copy)
    for n, copy in enumerate(sum_pushes):
        copy.wait_recv()
        total = total + sum_recv[n].astype(F32)
    out_ref[...] = total.astype(BF16)

    for copy in sum_pushes + [w_o_push, hidden_push]:
        copy.wait_send()
    for turn, copy in ab_pushes:
        if turn:
            copy.wait_send()
        else:
            pl.when(jnp.logical_not(is_root))(copy.wait_send)


def on_device(
    seq_count,
    head_count,
    tokens,
    w_query,
    w_key,
    w_value,
    w_beta,
    w_out,
    mask_query,
    mask_key,
    mask_value,
    mask_out,
    decay_rate,
    norm_gain,
):
    piece, width = tokens.shape
    span = piece * head_count
    value_cols = w_value.shape[1]
    in_cols = 2 * w_query.shape[1] + value_cols
    heads = value_cols // HD
    chips_x = seq_count // RING
    chips_y = head_count // CORES
    far_count = max(len(near_and_far(chips_y)[1]), 1) * CORES
    vmem = pl.BlockSpec(memory_space=pltpu.VMEM)
    hbm = pl.BlockSpec(memory_space=pltpu.HBM)
    dma = pltpu.SemaphoreType.DMA

    def in_hbm(array):
        return pltpu.with_memory_space_constraint(array, pltpu.HBM)

    made = pl.pallas_call(
        functools.partial(gather_kernel, head_count),
        out_shape=[
            pltpu.VMEM((head_count, piece, in_cols), BF16),
            pltpu.VMEM((head_count, piece, heads), F32),
            pltpu.VMEM((value_cols, width), BF16),
            pltpu.VMEM((heads, span), F32),
            pltpu.VMEM((span, HD), F32),
            pltpu.VMEM((heads, span, span), F32),
            pltpu.VMEM((span.bit_length(), span, span), BF16),
            pltpu.VMEM((far_count, piece, width), BF16),
            pltpu.VMEM((width, in_cols), BF16),
            pltpu.VMEM((heads, width), BF16),
        ],
        in_specs=[hbm] * 11,
        out_specs=[vmem] * 10,
        scratch_shapes=[
            pltpu.VMEM(mask_query.shape[::-1], jnp.int32),
            pltpu.VMEM(mask_key.shape[::-1], jnp.int32),
            pltpu.VMEM(mask_value.shape[::-1], jnp.int32),
            pltpu.VMEM(mask_out.shape, jnp.int32),
            pltpu.VMEM((heads, span), F32),
            pltpu.VMEM((head_count, piece, width), BF16),
            pltpu.VMEM((HD, span), F32),
            pltpu.VMEM((width // TILE, in_cols), F32),
            pltpu.VMEM((value_cols // TILE, width), F32),
            dma((4,)),
            dma((7,)),
            dma((chips_y,)),
            dma((chips_y,)),
            dma((chips_y,)),
            dma((chips_y,)),
        ],
        compiler_params=pltpu.CompilerParams(
            collective_id=0, has_side_effects=True, vmem_limit_bytes=40 * 1024 * 1024
        ),
        name="gather",
    )(
        *(
            in_hbm(array)
            for array in (
                tokens,
                w_query,
                w_key,
                w_value,
                w_beta.T,
                w_out,
                mask_query.T,
                mask_key.T,
                mask_value.T,
                mask_out,
                decay_rate.T,
            )
        )
    )
    return pl.pallas_call(
        functools.partial(state_kernel, seq_count, head_count),
        out_shape=pltpu.VMEM((piece, width), BF16),
        in_specs=[vmem] * 10 + [hbm],
        out_specs=vmem,
        scratch_shapes=[
            pltpu.VMEM((1, HD), F32),
            pltpu.VMEM((head_count, piece, in_cols), BF16),
            pltpu.VMEM((head_count, piece, heads), F32),
            pltpu.VMEM((value_cols, width), BF16),
            pltpu.VMEM((heads, span, HD), F32),
            pltpu.VMEM((heads, span, HD), BF16),
            pltpu.VMEM((heads, HD, 2 * HD), BF16),
            pltpu.VMEM((RING, HD, 2 * HD), BF16),
            pltpu.VMEM((HD, 2 * HD), BF16),
            pltpu.VMEM((chips_x, HD, 2 * HD), BF16),
            pltpu.VMEM((RING, HD, HD), BF16),
            pltpu.VMEM((heads, HD, HD), BF16),
            pltpu.VMEM((chips_y, CORES, piece, value_cols), BF16),
            pltpu.VMEM((chips_y, piece, value_cols), BF16),
            pltpu.VMEM((chips_y, piece, width), F32),
            pltpu.VMEM((chips_y - 1, piece, width), BF16),
            pltpu.VMEM((chips_y - 1, piece, width), BF16),
            dma((1,)),
            dma((heads,)),
            dma((RING,)),
            dma((chips_x,)),
            dma((chips_x,)),
            dma((RING,)),
            dma((heads,)),
            dma((2,)),
            dma((2,)),
            dma((chips_y - 1,)),
            dma((chips_y - 1,)),
        ],
        compiler_params=pltpu.CompilerParams(
            collective_id=1, has_side_effects=True, vmem_limit_bytes=40 * 1024 * 1024
        ),
        name="state",
    )(*made, in_hbm(norm_gain.reshape(1, HD)))


def solution(mesh):
    return jax.shard_map(
        functools.partial(on_device, mesh.shape["seq"], mesh.shape["head"]),
        mesh=mesh,
        in_specs=(
            P(("seq", "head"), None),
            P(None, "head"),
            P(None, "head"),
            P(None, "head"),
            P(None, "head"),
            P("head", None),
            P(None, "head"),
            P(None, "head"),
            P(None, "head"),
            P("head", None),
            P("seq", "head"),
            P(),
        ),
        out_specs=P(("seq", "head"), None),
        check_vma=False,
    )
```

```python
import functools
import math

import jax
import jax.numpy as jnp
from jax import lax
from jax.experimental import pallas as pl
from jax.experimental.pallas import tpu as pltpu
from jax.sharding import PartitionSpec as P

HD = 128
TILE = 64
RING = 8
CORES = 2
COLUMN_PARTS = 2
MESH = pl.DeviceIdType.MESH
F32 = jnp.float32
BF16 = jnp.bfloat16


def mm(left, right):
    return jnp.dot(left.astype(BF16), right.astype(BF16), preferred_element_type=F32)


def mm_nt(left, right):
    return lax.dot_general(
        left, right, (((1,), (1,)), ((), ())), preferred_element_type=F32
    )


def unit_rows(matrix):
    return matrix * lax.rsqrt(jnp.sum(matrix * matrix, -1, keepdims=True) + 1e-06)


def spread_blocks(columns, count):
    rows = columns.shape[0]
    first = lax.broadcasted_iota(jnp.int32, (rows, 2 * TILE), 1) < TILE
    return jnp.concatenate(
        [
            jnp.where(first, columns[:, 2 * i : 2 * i + 1], columns[:, 2 * i + 1 : 2 * i + 2])
            for i in range(count // 2)
        ],
        axis=1,
    )


def corner_masks(row, col):
    masks = [row == col]
    shift = 0
    while (1 << shift) < row.shape[0]:
        masks.append(
            ((row >> (shift + 1)) == (col >> (shift + 1))) & ((row >> shift) != (col >> shift)) & (row > col)
        )
        shift += 1
    return masks


def unit_lower_inverses(negated, masks):
    inverses = [masks[0] + lower * masks[1] for lower in negated]
    for n in range(2, masks.shape[0]):
        corner = masks[n]
        halves = [mm(inverse, lower * corner).astype(BF16) for inverse, lower in zip(inverses, negated)]
        inverses = [inverse + mm(half, inverse).astype(BF16) for inverse, half in zip(inverses, halves)]
    return inverses


def push(source, target, send_sem, recv_sem, device):
    return pltpu.make_async_remote_copy(
        src_ref=source,
        dst_ref=target,
        send_sem=send_sem,
        recv_sem=recv_sem,
        device_id=device,
        device_id_type=MESH,
    )


def greet(partners):
    barrier = pltpu.get_barrier_semaphore()
    for partner in partners:
        pl.semaphore_signal(barrier, inc=1, device_id=partner, device_id_type=MESH)
    return lambda: pl.semaphore_wait(barrier, len(partners))


def far_first_steps(count):
    return sorted(range(1, count), key=lambda step: -min(step, count - step))


def near_and_far(chips_y):
    steps = far_first_steps(chips_y)
    far = [step for step in steps if min(step, chips_y - step) > 1]
    return [step for step in steps if step not in far], far


def chip_slots(y, chips_y, steps):
    return [lax.rem(y + chips_y - step, chips_y) * CORES + core for step in steps for core in range(CORES)]


def project(rows, w_in, w_beta, key_cols):
    raw = jnp.dot(rows, w_in[...], preferred_element_type=F32)
    beta = jax.nn.sigmoid(mm_nt(rows, w_beta[...]))
    parts = []
    for at in range(0, key_cols, HD):
        parts.append((unit_rows(raw[:, at : at + HD]) * (1.0 / math.sqrt(HD))).astype(BF16))
    for at in range(key_cols, 2 * key_cols, HD):
        parts.append(unit_rows(raw[:, at : at + HD]).astype(BF16))
    parts.append(jax.nn.silu(raw[:, 2 * key_cols :]).astype(BF16))
    return jnp.concatenate(parts, axis=1), beta


def gather_kernel(
    head_count,
    tokens_ref,
    w_query_ref,
    w_key_ref,
    w_value_ref,
    w_beta_hbm,
    w_out_ref,
    mask_query_hbm,
    mask_key_hbm,
    mask_value_hbm,
    mask_out_hbm,
    decay_hbm,
    qkv,
    beta_out,
    w_o,
    log_rows_ref,
    columns_ref,
    decays_ref,
    masks_ref,
    far_rows,
    w_in,
    w_beta_ref,
    mask_query_ref,
    mask_key_ref,
    mask_value_ref,
    mask_out_ref,
    decay_ref,
    tok,
    small,
    rows_in,
    rows_out,
    w_sem,
    small_sem,
    tok_send_sem,
    tok_recv_sem,
    sib_send_sem,
    sib_recv_sem,
):
    s = lax.axis_index("seq")
    hd = lax.axis_index("head")
    chips_y = head_count // CORES
    y, core = hd // CORES, lax.rem(hd, CORES)
    piece, width = tokens_ref.shape
    span = piece * head_count
    key_cols = w_query_ref.shape[1]
    value_cols = w_value_ref.shape[1]
    heads = value_cols // HD
    key_heads = key_cols // HD
    in_cols = 2 * key_cols + value_cols

    def at_y(step):
        return (s, lax.rem(y + step, chips_y) * CORES + core)

    sibling = (s, y * CORES + (1 - core))
    far_first = far_first_steps(chips_y)
    wait_partners = greet([at_y(step) for step in range(1, chips_y)] + [sibling])

    small_copies = [
        pltpu.make_async_copy(source, target, small_sem.at[n])
        for n, (source, target) in enumerate(
            (
                (mask_query_hbm, mask_query_ref),
                (mask_key_hbm, mask_key_ref),
                (mask_value_hbm, mask_value_ref),
                (mask_out_hbm, mask_out_ref),
                (w_beta_hbm, w_beta_ref),
                (decay_hbm, decay_ref),
                (tokens_ref, tok.at[hd]),
            )
        )
    ]
    for copy in small_copies:
        copy.start()
    weight_copies = [
        pltpu.make_async_copy(w_query_ref, w_in.at[:, pl.ds(0, key_cols)], w_sem.at[0]),
        pltpu.make_async_copy(w_key_ref, w_in.at[:, pl.ds(key_cols, key_cols)], w_sem.at[1]),
        pltpu.make_async_copy(w_value_ref, w_in.at[:, pl.ds(2 * key_cols, value_cols)], w_sem.at[2]),
        pltpu.make_async_copy(w_out_ref, w_o, w_sem.at[3]),
    ]
    for copy in weight_copies:
        copy.start()
    wait_partners()

    token_pushes = {
        step: push(
            tokens_ref, tok.at[hd], tok_send_sem.at[step], tok_recv_sem.at[step], at_y(step)
        )
        for step in far_first
    }
    for step in reversed(far_first):
        token_pushes[step].start()
    sibling_pushes = {
        0: push(tokens_ref, tok.at[hd], sib_send_sem.at[0], sib_recv_sem.at[0], sibling)
    }
    sibling_pushes[0].start()

    for copy in small_copies:
        copy.wait()
    small[...] = jnp.zeros_like(small)
    mask_blocks = 0
    for ref in (mask_query_ref, mask_key_ref, mask_value_ref):
        small[mask_blocks : mask_blocks + ref.shape[0], 0 : ref.shape[1]] = ref[...].astype(F32)
        mask_blocks += ref.shape[0]
    turned = jnp.transpose(small[:, 0:HD])
    rows_in[...] = spread_blocks(turned[0 : rows_in.shape[0], :], mask_blocks)
    rows_out[...] = spread_blocks(mask_out_ref[...].astype(F32), mask_out_ref.shape[1])

    def mask_tiles(weight, rows):
        def step(i, carry):
            at = pl.ds(pl.multiple_of(i * TILE, TILE), TILE)
            kept = jnp.broadcast_to(rows[pl.ds(i, 1), :], (16, rows.shape[1])).astype(BF16)
            tile = weight[at, :].reshape(TILE // 16, 16, rows.shape[1])
            weight[at, :] = (tile * kept[None]).reshape(TILE, rows.shape[1])
            return carry

        lax.fori_loop(0, rows.shape[0], step, 0)

    for copy in weight_copies[:3]:
        copy.wait()
    mask_tiles(w_in, rows_in)
    weight_copies[3].wait()
    mask_tiles(w_o, rows_out)

    row = lax.broadcasted_iota(jnp.int32, (span, span), 0)
    col = lax.broadcasted_iota(jnp.int32, (span, span), 1)
    log_rows = jnp.dot(
        jnp.log(decay_ref[...]),
        jnp.where(row <= col, 1.0, 0.0),
        precision=lax.Precision.HIGHEST,
        preferred_element_type=F32,
    )
    small[0:heads, :] = log_rows
    columns = jnp.transpose(small[...])
    log_rows_ref[...] = log_rows
    columns_ref[...] = columns

    def forward(step):
        token_pushes[step].wait_recv()
        held = tok.at[lax.rem(y + chips_y - step, chips_y) * CORES + core]
        copy = push(held, held, sib_send_sem.at[step], sib_recv_sem.at[step], sibling)
        copy.start()
        sibling_pushes[step] = copy

    def slots_of(steps):
        return chip_slots(y, chips_y, steps)

    near, far = near_and_far(chips_y)
    for step in near:
        forward(step)
    for n, mask in enumerate(corner_masks(row, col)):
        masks_ref[n] = jnp.where(mask, 1.0, 0.0).astype(BF16)
    for h in range(heads):
        spread = jnp.where(row >= col, columns[:, h : h + 1] - log_rows[h : h + 1, :], 0.0)
        decays_ref[h] = jnp.where(row >= col, jnp.exp(spread), 0.0)
    for step in far:
        forward(step)
    for step in [0] + near:
        sibling_pushes[step].wait_recv()
    slots = slots_of([0] + near)
    rows = jnp.concatenate([tok[slot] for slot in slots], axis=0)
    made, beta = project(rows, w_in, w_beta_ref, key_cols)
    for n, slot in enumerate(slots):
        qkv[slot] = made[n * piece : (n + 1) * piece]
        beta_out[slot] = beta[n * piece : (n + 1) * piece]
    for step in far:
        sibling_pushes[step].wait_recv()
    for n, slot in enumerate(slots_of(far)):
        far_rows[n] = tok[slot]

    for step in far_first:
        token_pushes[step].wait_send()
    for copy in sibling_pushes.values():
        copy.wait_send()


def state_kernel(
    seq_count,
    head_count,
    qkv,
    beta_out,
    w_o,
    log_rows_ref,
    columns_ref,
    decays_ref,
    masks_ref,
    far_rows,
    w_in,
    w_beta_ref,
    gain_hbm,
    out_ref,
    gain_ref,
    qkv_all,
    beta_all,
    w_o_other,
    local_out,
    local_q,
    ab_send,
    ab_recv,
    x_send,
    x_recv,
    s_send,
    s_recv,
    hidden,
    hidden_other,
    own_part,
    sum_send,
    sum_recv,
    small_sem,
    ab_send_sem,
    ab_recv_sem,
    x_send_sem,
    x_recv_sem,
    s_send_sem,
    s_recv_sem,
    other_send_sem,
    other_recv_sem,
    sum_send_sem,
    sum_recv_sem,
):
    s = lax.axis_index("seq")
    hd = lax.axis_index("head")
    chips_x = seq_count // RING
    chips_y = head_count // CORES
    x, z = s // RING, lax.rem(s, RING)
    y, core = hd // CORES, lax.rem(hd, CORES)
    _, piece, in_cols = qkv.shape
    value_cols, width = w_o.shape
    span = piece * head_count
    key_cols = (in_cols - value_cols) // 2
    heads = value_cols // HD
    key_heads = key_cols // HD

    def at_y(step):
        return (s, lax.rem(y + step, chips_y) * CORES + core)

    sibling = (s, y * CORES + (1 - core))

    def at_z(place):
        return (x * RING + place, hd)

    def at_x(step):
        return (lax.rem(x + step, chips_x) * RING + z, hd)

    far_first = far_first_steps(chips_y)
    far_first_x = far_first_steps(chips_x)
    wait_partners = greet(
        [at_z(lax.rem(z + step, RING)) for step in far_first_steps(RING)]
        + [at_x(step) for step in far_first_x]
        + [at_y(step) for step in far_first]
        + [sibling]
    )
    gain_copy = pltpu.make_async_copy(gain_hbm, gain_ref, small_sem.at[0])
    gain_copy.start()
    row = lax.broadcasted_iota(jnp.int32, (span, span), 0)
    col = lax.broadcasted_iota(jnp.int32, (span, span), 1)
    log_rows = log_rows_ref[...]
    columns = columns_ref[...]

    qkv_all[...] = qkv[...]
    beta_all[...] = beta_out[...]
    _, far = near_and_far(chips_y)
    if far:
        slots = chip_slots(y, chips_y, far)
        rows = far_rows[...].reshape(len(slots) * piece, width)
        made, beta = project(rows, w_in, w_beta_ref, key_cols)
        for n, slot in enumerate(slots):
            qkv_all[slot] = made[n * piece : (n + 1) * piece]
            beta_all[slot] = beta[n * piece : (n + 1) * piece]
    made = qkv_all[...].reshape(span, in_cols)
    beta_cols = beta_all[...].reshape(span, heads)
    queries, keys, key_turned, grams, pair_scores = [], [], [], [], []
    for i in range(key_heads):
        query = made[:, i * HD : (i + 1) * HD]
        key = made[:, key_cols + i * HD : key_cols + (i + 1) * HD]
        queries.append(query.astype(F32))
        keys.append(key.astype(F32))
        key_turned.append(jnp.transpose(key.astype(F32)))
        grams.append(mm_nt(key, key))
        pair_scores.append(mm_nt(query, key))
    values = made[:, 2 * key_cols : in_cols].astype(F32)

    eye = jnp.where(
        lax.broadcasted_iota(jnp.int32, (HD, HD), 0) == lax.broadcasted_iota(jnp.int32, (HD, HD), 1),
        1.0,
        0.0,
    )
    is_root = lax.rem(z, CORES) == core

    def key_head(h):
        return h * key_heads // heads

    ab_pushes = []
    far_first_heads = sorted(range(heads), key=lambda turn: -min(turn, heads - turn))
    members = range(heads)
    lasts = [log_rows[h : h + 1, span - 1 : span] for h in members]
    rises = [jnp.exp(columns[:, h : h + 1]) for h in members]
    betas = [beta_cols[:, h : h + 1] for h in members]
    decays = [decays_ref[h] for h in members]
    inverses = unit_lower_inverses(
        [
            jnp.where(row > col, -beta * decay * grams[key_head(h)], 0.0).astype(BF16)
            for h, beta, decay in zip(members, betas, decays)
        ],
        masks_ref,
    )
    mixes = [
        mm(
            inverse,
            jnp.concatenate(
                [
                    ((beta * rise) * keys[key_head(h)]).astype(BF16),
                    (beta * values[:, h * HD : (h + 1) * HD]).astype(BF16),
                ],
                axis=1,
            ),
        ).astype(BF16)
        for h, inverse, beta, rise in zip(members, inverses, betas, rises)
    ]
    ends = [
        mm(key_turned[key_head(h)] * jnp.exp(last - log_rows[h : h + 1, :]), mixed)
        for h, last, mixed in zip(members, lasts, mixes)
    ]
    for h, last, end in zip(members, lasts, ends):
        transition = jnp.exp(last) * eye - end[:, 0:HD]
        ab_send[h] = jnp.concatenate([transition, end[:, HD : 2 * HD]], axis=1).astype(BF16)

    wait_partners()
    for turn in far_first_heads:
        h = lax.rem(z // CORES + turn, heads)
        target = h * CORES + core
        copy = push(ab_send.at[h], ab_recv.at[z], ab_send_sem.at[turn], ab_recv_sem.at[z], at_z(target))
        ab_pushes.append((turn, copy))
        if turn:
            copy.start()
        else:
            pl.when(jnp.logical_not(is_root))(copy.start)

    @pl.when(is_root)
    def _():
        ab_recv[z] = ab_send[z // CORES]

    w_o_push = push(w_o, w_o_other, other_send_sem.at[0], other_recv_sem.at[0], sibling)
    w_o_push.start()

    reads = [
        mm(pair_scores[key_head(h)] * decay, mixed) for h, decay, mixed in zip(members, decays, mixes)
    ]
    for h, rise, read in zip(members, rises, reads):
        local_out[h] = read[:, HD : 2 * HD]
        local_q[h] = (rise * queries[key_head(h)] - read[:, 0:HD]).astype(BF16)

    def ring_step(step):
        return lax.rem(z + step, RING)

    def s_push(step):
        mine, place = z // CORES, ring_step(step)
        return push(
            s_send.at[place], s_recv.at[mine], s_send_sem.at[step], s_recv_sem.at[mine], at_z(place)
        )

    def after(later, earlier):
        both = mm(later[:, 0:HD], earlier)
        return jnp.concatenate(
            [both[:, 0:HD], both[:, HD : 2 * HD] + later[:, HD : 2 * HD].astype(F32)], axis=1
        )

    def advance(pair, state):
        return mm(pair[:, 0:HD], state) + pair[:, HD : 2 * HD].astype(F32)

    far_first_z = far_first_steps(RING)

    @pl.when(is_root)
    def _():
        for step in reversed(far_first_z):
            place = ring_step(step)
            push(
                ab_send.at[0], ab_recv.at[place], ab_send_sem.at[0], ab_recv_sem.at[place], at_z(place)
            ).wait_recv()
        pairs = [ab_recv[place] for place in range(RING)]
        level = {(place, place + 1): pairs[place] for place in range(RING)}
        size = 1
        while size < RING:
            for low in range(0, RING, 2 * size):
                level[low, low + 2 * size] = after(
                    level[low + size, low + 2 * size], level[low, low + size]
                ).astype(BF16)
            size *= 2
        x_send[...] = level[0, RING]
        x_pushes = {
            step: push(x_send, x_recv.at[x], x_send_sem.at[step], x_recv_sem.at[step], at_x(step))
            for step in far_first_x
        }
        for step, copy in x_pushes.items():
            pl.when(x + step < chips_x)(copy.start)
        prefixes = []
        for end in range(1, RING):
            low, total = 0, None
            for size in (4, 2, 1):
                if end & size:
                    part = level[low, low + size]
                    total = part if total is None else after(part, total).astype(BF16)
                    low += size
            prefixes.append(total)
        for step in far_first_x:
            earlier = push(
                x_send, x_recv.at[x - step], x_send_sem.at[step], x_recv_sem.at[step], at_x(step)
            )
            pl.when(x >= step)(earlier.wait_recv)
        state = jnp.where(x > 0, x_recv[0, :, HD : 2 * HD].astype(F32), 0.0)
        for place in range(1, chips_x - 1):
            state = jnp.where(place < x, advance(x_recv[place], state), state)
        s_send[0] = state.astype(BF16)
        for place in range(1, RING):
            s_send[place] = advance(prefixes[place - 1], state).astype(BF16)
        for step in far_first_z:
            s_push(step).start()
        s_recv[z // CORES] = s_send[z]
        for step, copy in x_pushes.items():
            pl.when(x + step < chips_x)(copy.wait_send)
        for step in far_first_z:
            s_push(step).wait_send()

    gain_copy.wait()
    for h in range(heads):
        source = h * CORES + core

        @pl.when(z != source)
        def _():
            push(
                s_send.at[0], s_recv.at[h], s_send_sem.at[0], s_recv_sem.at[h], at_z(source)
            ).wait_recv()

        state_out = local_out[h] + jnp.dot(local_q[h], s_recv[h], preferred_element_type=F32)
        inv_rms = lax.rsqrt(jnp.mean(state_out * state_out, -1, keepdims=True) + 1e-06)
        hidden[:, :, :, h * HD : (h + 1) * HD] = (
            (state_out * inv_rms * gain_ref[...]).astype(BF16).reshape(chips_y, CORES, piece, HD)
        )

    hidden_push = push(
        hidden.at[:, 1 - core], hidden_other, other_send_sem.at[1], other_recv_sem.at[1], sibling
    )
    hidden_push.start()
    order = far_first + [0]
    places = [lax.rem(y + step, chips_y) for step in order]
    own_rows = jnp.concatenate([hidden[place, core] for place in places], axis=0)
    own_part[...] = jnp.dot(own_rows, w_o[...], preferred_element_type=F32).reshape(chips_y, piece, width)
    w_o_push.wait_recv()
    hidden_push.wait_recv()
    sum_pushes = []
    rows = jnp.concatenate([hidden_other[place] for place in places], axis=0)
    part = width // COLUMN_PARTS
    for first in range(0, width, part):
        at = slice(first, first + part)
        both = jnp.dot(rows, w_o_other[:, at], preferred_element_type=F32).reshape(chips_y, piece, part)
        both = both + own_part[:, :, at]
        for n, step in enumerate(order):
            if step == 0:
                own_part[n, :, at] = both[n]
            else:
                sum_send[n, :, at] = both[n].astype(BF16)
                sem = len(sum_pushes)
                columns_at = pl.ds(first, part)
                copy = push(
                    sum_send.at[n, :, columns_at],
                    sum_recv.at[n, :, columns_at],
                    sum_send_sem.at[sem],
                    sum_recv_sem.at[sem],
                    at_y(step),
                )
                copy.start()
                sum_pushes.append(copy)
    for copy in sum_pushes:
        copy.wait_recv()
    total = own_part[len(order) - 1]
    for n in range(len(order) - 1):
        total = total + sum_recv[n].astype(F32)
    out_ref[...] = total.astype(BF16)

    for copy in sum_pushes + [w_o_push, hidden_push]:
        copy.wait_send()
    for turn, copy in ab_pushes:
        if turn:
            copy.wait_send()
        else:
            pl.when(jnp.logical_not(is_root))(copy.wait_send)


def on_device(
    seq_count,
    head_count,
    tokens,
    w_query,
    w_key,
    w_value,
    w_beta,
    w_out,
    mask_query,
    mask_key,
    mask_value,
    mask_out,
    decay_rate,
    norm_gain,
):
    piece, width = tokens.shape
    span = piece * head_count
    value_cols = w_value.shape[1]
    in_cols = 2 * w_query.shape[1] + value_cols
    heads = value_cols // HD
    chips_x = seq_count // RING
    chips_y = head_count // CORES
    far_count = max(len(near_and_far(chips_y)[1]), 1) * CORES
    vmem = pl.BlockSpec(memory_space=pltpu.VMEM)
    hbm = pl.BlockSpec(memory_space=pltpu.HBM)
    dma = pltpu.SemaphoreType.DMA

    def in_hbm(array):
        return pltpu.with_memory_space_constraint(array, pltpu.HBM)

    made = pl.pallas_call(
        functools.partial(gather_kernel, head_count),
        out_shape=[
            pltpu.VMEM((head_count, piece, in_cols), BF16),
            pltpu.VMEM((head_count, piece, heads), F32),
            pltpu.VMEM((value_cols, width), BF16),
            pltpu.VMEM((heads, span), F32),
            pltpu.VMEM((span, HD), F32),
            pltpu.VMEM((heads, span, span), F32),
            pltpu.VMEM((span.bit_length(), span, span), BF16),
            pltpu.VMEM((far_count, piece, width), BF16),
            pltpu.VMEM((width, in_cols), BF16),
            pltpu.VMEM((heads, width), BF16),
        ],
        in_specs=[hbm] * 11,
        out_specs=[vmem] * 10,
        scratch_shapes=[
            pltpu.VMEM(mask_query.shape[::-1], jnp.int32),
            pltpu.VMEM(mask_key.shape[::-1], jnp.int32),
            pltpu.VMEM(mask_value.shape[::-1], jnp.int32),
            pltpu.VMEM(mask_out.shape, jnp.int32),
            pltpu.VMEM((heads, span), F32),
            pltpu.VMEM((head_count, piece, width), BF16),
            pltpu.VMEM((HD, span), F32),
            pltpu.VMEM((width // TILE, in_cols), F32),
            pltpu.VMEM((value_cols // TILE, width), F32),
            dma((4,)),
            dma((7,)),
            dma((chips_y,)),
            dma((chips_y,)),
            dma((chips_y,)),
            dma((chips_y,)),
        ],
        compiler_params=pltpu.CompilerParams(
            collective_id=0, has_side_effects=True, vmem_limit_bytes=40 * 1024 * 1024
        ),
        name="gather",
    )(
        *(
            in_hbm(array)
            for array in (
                tokens,
                w_query,
                w_key,
                w_value,
                w_beta.T,
                w_out,
                mask_query.T,
                mask_key.T,
                mask_value.T,
                mask_out,
                decay_rate.T,
            )
        )
    )
    return pl.pallas_call(
        functools.partial(state_kernel, seq_count, head_count),
        out_shape=pltpu.VMEM((piece, width), BF16),
        in_specs=[vmem] * 10 + [hbm],
        out_specs=vmem,
        scratch_shapes=[
            pltpu.VMEM((1, HD), F32),
            pltpu.VMEM((head_count, piece, in_cols), BF16),
            pltpu.VMEM((head_count, piece, heads), F32),
            pltpu.VMEM((value_cols, width), BF16),
            pltpu.VMEM((heads, span, HD), F32),
            pltpu.VMEM((heads, span, HD), BF16),
            pltpu.VMEM((heads, HD, 2 * HD), BF16),
            pltpu.VMEM((RING, HD, 2 * HD), BF16),
            pltpu.VMEM((HD, 2 * HD), BF16),
            pltpu.VMEM((chips_x, HD, 2 * HD), BF16),
            pltpu.VMEM((RING, HD, HD), BF16),
            pltpu.VMEM((heads, HD, HD), BF16),
            pltpu.VMEM((chips_y, CORES, piece, value_cols), BF16),
            pltpu.VMEM((chips_y, piece, value_cols), BF16),
            pltpu.VMEM((chips_y, piece, width), F32),
            pltpu.VMEM((chips_y - 1, piece, width), BF16),
            pltpu.VMEM((chips_y - 1, piece, width), BF16),
            dma((1,)),
            dma((heads,)),
            dma((RING,)),
            dma((chips_x,)),
            dma((chips_x,)),
            dma((RING,)),
            dma((heads,)),
            dma((2,)),
            dma((2,)),
            dma((COLUMN_PARTS * (chips_y - 1),)),
            dma((COLUMN_PARTS * (chips_y - 1),)),
        ],
        compiler_params=pltpu.CompilerParams(
            collective_id=1, has_side_effects=True, vmem_limit_bytes=40 * 1024 * 1024
        ),
        name="state",
    )(*made, in_hbm(norm_gain.reshape(1, HD)))


def solution(mesh):
    return jax.shard_map(
        functools.partial(on_device, mesh.shape["seq"], mesh.shape["head"]),
        mesh=mesh,
        in_specs=(
            P(("seq", "head"), None),
            P(None, "head"),
            P(None, "head"),
            P(None, "head"),
            P(None, "head"),
            P("head", None),
            P(None, "head"),
            P(None, "head"),
            P(None, "head"),
            P("head", None),
            P("seq", "head"),
            P(),
        ),
        out_specs=P(("seq", "head"), None),
        check_vma=False,
    )
```
